128 devices in a mesh: rows: 8 (over z, core), cols: 16 (over y, x).
Axes of the slice: x: 4, y: 4, z: 4, core: 2. Of those that a mesh axis runs over, the one named last changes fastest.
Arguments:
- estimate: float32 [4, 147456], P(None, 'cols'), may hold values from -6 to 6
- dark_hole: int32 [4096], replicated, may hold values from 0 to 147455, as said below
- jacobian: float32 [16384, 18432], P('rows', 'cols'), may hold values from -0.046875 to 0.046875
- basis: float32 [18432, 18432], P('rows', 'cols'), may hold values from -0.046875 to 0.046875
- eigenvalues: float32 [18432], P('rows'), may hold values from 0.5 to 8
- exponents: int32 [8], replicated, may hold values from -2 to 3
- wavelengths: float32 [12], replicated, may hold values from 0.9 to 1.1
- amplitude: float32 [256, 256], replicated, may hold values from 0.2 to 1
- aberration: float32 [256, 256], replicated, may hold values from -3 to 3
- influence: float32 [2, 256, 96], replicated, may hold values from -0.625 to 0.625
Outputs:
- commands: float32 [8, 18432], P(None, 'cols')
- image: float32 [96, 384, 384], P('cols', 'rows')
- contrast: float32 [16, 6], P('cols')
The draws below stay inside these ranges and needn't reach their ends.
Inputs may be any that keep to these rules, and one draw needn't show every extreme that they name: `dark_hole`: 4096 distinct indices; the first is 0 and the last 147455.
All inputs are finite; a program needn't handle non-finite values.
Results may differ from the reference program's by a relative error of at most 0.0003.
Values sent between devices are 32-bit elements; how exact they have to be, the bound alone decides.
No kernel may reach another device: no remote copies, remote signals or barrier semaphores. Data moves between devices by JAX's collectives and lax.ppermute only.
A program may use at most 64 MiB of HBM per device.

```python
import math
import jax
import jax.numpy as jnp
from jax import lax

ACT = 96
NA = 18432
EST_WAVES = 2
ROWS = 16384
DH = 4096
FP = 384
FPIX = 147456
PUP = 256
CANDS = 8
WAVES = 12
GROUPS = 2
WPD = 6


def draw_dark_hole(key, part):
    key = jax.random.fold_in(key, 11)
    interior = jax.random.permutation(key, FP * FP - 2)[:DH - 2].astype(jnp.int32) + 1
    first_index = jnp.zeros((1,), jnp.int32)
    last_index = jnp.full((1,), FP * FP - 1, jnp.int32)
    return jnp.concatenate([first_index, interior, last_index])


def set_ends(drawn, stream_key, least, top_value):
    longest = drawn.shape.index(max(drawn.shape))
    spots = []
    for shift in (0, 1):
        where = [jax.random.randint(jax.random.fold_in(stream_key, axis), (), 0, length) for axis, length in enumerate(drawn.shape)]
        where[longest] = (where[longest] + shift) % drawn.shape[longest]
        spots.append(tuple(where))
    return drawn.at[spots[0]].set(least).at[spots[1]].set(top_value)


def shard_levels(rng, dims, split, smallest, high):
    factor_of, own = 1.0, jax.random.fold_in(rng, 6)
    for dim, shards_of in split:
        steps = jnp.exp(jax.random.uniform(jax.random.fold_in(own, dim), (shards_of,), jnp.float32, smallest / len(split), high / len(split)))
        factor_of = factor_of * jnp.repeat(steps, dims[dim] // shards_of).reshape([-1 if axis == dim else 1 for axis in range(len(dims))])
    return factor_of


def scatter_about(own_key, dims, width, most, split=(), held_as=jnp.bfloat16):
    drawn = width * jax.random.normal(own_key, dims, jnp.float32)
    if split:
        drawn = drawn * shard_levels(own_key, dims, split, -0.22, 0.18)
    return jnp.clip(drawn, -most, most).astype(held_as)


def setup_inputs(seed: int = 0) -> dict:
    splits = jax.random.split(jax.random.key(seed), 11)
    return {
        "estimate": scatter_about(splits[0], (2 * EST_WAVES, FPIX), 1.0, 6.0, ((1, 16),), jnp.float32),
        "dark_hole": draw_dark_hole(jax.random.fold_in(splits[10], 71), 0),
        "jacobian": scatter_about(splits[2], (ROWS, NA), ROWS ** -0.5, 0.046875, ((0, 8), (1, 16)), jnp.float32),
        "basis": scatter_about(splits[3], (NA, NA), NA ** -0.5, 0.046875, ((0, 8), (1, 16)), jnp.float32),
        "eigenvalues": jnp.clip(jnp.exp(math.log(8.0) - 2.7725887 * jax.random.uniform(splits[4], (NA,), jnp.float32) ** shard_levels(splits[4], (NA,), ((0, 8),), -0.2, 0.2)), 0.5, 8.0),
        "exponents": set_ends(jax.random.randint(splits[5], (CANDS,), -2, 4), jax.random.fold_in(splits[5], 1), -2, 3).astype(jnp.int32),
        "wavelengths": jnp.clip(jnp.exp(jax.random.uniform(splits[6], (WAVES,), jnp.float32, math.log(0.9), math.log(1.1))), 0.9, 1.1),
        "amplitude": jnp.clip(jax.random.uniform(splits[7], (PUP, PUP), jnp.float32, 0.2, 1.0), 0.2, 1.0),
        "aberration": scatter_about(splits[8], (PUP, PUP), 0.5, 3.0, (), jnp.float32),
        "influence": scatter_about(splits[9], (2, PUP, ACT), ACT ** -0.5, 0.625, (), jnp.float32),
    }


EPSILON = 1e-6
STROKE = 0.05
PIXEL_SCALE = 0.25
TWO_PI = 2.0 * math.pi


def product(left, right):
    return jnp.dot(left, right, precision=lax.Precision.HIGHEST, preferred_element_type=jnp.float32)


def transform_table(positions, wavelength, focal_size, pupil_size):
    freq = (positions - (focal_size / 2 - 0.5)) * (PIXEL_SCALE / wavelength)
    place = (jnp.arange(pupil_size, dtype=jnp.int32).astype(jnp.float32) - (pupil_size / 2 - 0.5)) / pupil_size
    angle = (-TWO_PI) * freq[:, None] * place[None, :]
    return jnp.cos(angle), jnp.sin(angle)


def dm_surface(command, influence):
    acts = influence.shape[2]
    actuators = command.reshape(2, acts, acts)
    summed = product(product(influence[0], actuators[0]), influence[0].T)
    left_part = product(influence[1], actuators[1])
    return summed + product(left_part, influence[1].T)


def focal_intensity(field_re, field_im, table_y, table_x):
    pupil_size = field_re.shape[1]
    stacked_pupil = jnp.concatenate([field_re, field_im], axis=1)
    upper_part = product(table_y[0], stacked_pupil)
    second = product(table_y[1], stacked_pupil)
    middle_re = upper_part[:, :pupil_size] - second[:, pupil_size:]
    middle_im = upper_part[:, pupil_size:] + second[:, :pupil_size]
    stacked_mid = jnp.concatenate([middle_re, middle_im], axis=0)
    right_side = jnp.concatenate([table_x[0].T, table_x[1].T], axis=1)
    outer_product = product(stacked_mid, right_side)
    rows_count = middle_re.shape[0]
    focal_size = table_x[0].shape[0]
    focal_re = outer_product[:rows_count, :focal_size] - outer_product[rows_count:, focal_size:]
    focal_im = outer_product[:rows_count, focal_size:] + outer_product[rows_count:, :focal_size]
    return focal_re * focal_re + focal_im * focal_im


def reference(estimate, dark_hole, jacobian, basis, eigenvalues, exponents, wavelengths, amplitude, aberration, influence):
    field_rows = estimate[:, dark_hole].reshape(-1)
    gradient = product(field_rows[None, :], jacobian)[0]
    modal_coeffs = product(basis, gradient[:, None])[:, 0]
    damping = jnp.power(2.0, exponents.astype(jnp.float32))
    weights = -modal_coeffs[None, :] / (eigenvalues[None, :] + damping[:, None])
    commands = product(weights, basis)
    pupil_size = amplitude.shape[0]
    positions = jnp.arange(FP, dtype=jnp.int32).astype(jnp.float32)

    def check(pair):
        cand = pair // WAVES
        wave = pair % WAVES
        wavelength = wavelengths[wave]
        chosen = lax.dynamic_index_in_dim(commands, cand, 0, keepdims=False)
        height = aberration + (2.0 * STROKE) * dm_surface(chosen, influence)
        phase = (TWO_PI / wavelength) * height
        table = transform_table(positions, wavelength, FP, pupil_size)
        return focal_intensity(amplitude * jnp.cos(phase), amplitude * jnp.sin(phase), table, table)

    intensity = lax.map(check, jnp.arange(CANDS * WAVES, dtype=jnp.int32))
    flat = intensity.reshape(CANDS * WAVES, FP * FP)
    summed = jnp.sum(flat, axis=1)
    hole_sum = jnp.sum(flat[:, dark_hole], axis=1)
    scale = summed / (FP * FP) + EPSILON
    image = intensity / scale[:, None, None]
    contrast = (hole_sum / dark_hole.shape[0]) / scale
    return commands, image, contrast.reshape(CANDS * GROUPS, WPD)
```

```python
import functools

import jax
import jax.numpy as jnp
from jax import lax
from jax.experimental import pallas as pl
from jax.experimental.pallas import tpu as pltpu
from jax.sharding import PartitionSpec as P

FP = 384
PUP = 256
ACT = 96
LANES = 128
EPSILON = 1e-6
STROKE = 0.05
PIXEL_SCALE = 0.25
F32 = jnp.float32
BF16 = jnp.bfloat16
HIGHEST = lax.Precision.HIGHEST

COS = (1.0, -19.73920440673828, 64.93911743164062, -85.45014190673828, 60.16762924194336, -25.967599868774414, 6.528658390045166)
SIN = (6.2831854820251465, -41.34170150756836, 81.60513305664062, -76.70301818847656, 42.02592849731445, -14.899847030639648, 3.2381374835968018)


def horner(coefs, x):
    acc = jnp.full_like(x, coefs[-1])
    for c in coefs[-2::-1]:
        acc = acc * x + c
    return acc


def cos_sin_turns(t):
    r = t - jnp.round(t)
    x = r * r
    return horner(COS, x), horner(SIN, x) * r


def split2(x):
    hi = x.astype(BF16)
    return hi, (x - hi.astype(F32)).astype(BF16)


def mm(a, b):
    return jnp.dot(a, b, preferred_element_type=F32)


def mm_t(a, b, precision=None):
    return lax.dot_general(a, b, (((1,), (1,)), ((), ())), preferred_element_type=F32, precision=precision)


def tdot(a, b):
    return lax.dot_general(a, b, (((0,), (0,)), ((), ())), preferred_element_type=F32)


def spread(ref, row):
    for j in range(ref.shape[0]):
        ref[j] = row


def gathered_sum(ref):
    total = ref[0]
    for j in range(1, ref.shape[0]):
        total = total + ref[j]
    return total


def pick_kernel(est_ref, dh_ref, out_ref, mask_ref, table_ref, flat_ref):
    row = lax.axis_index("rows")
    col = lax.axis_index("cols")
    rows = lax.axis_size("rows")
    planes, width = est_ref.shape
    count = out_ref.shape[-1]
    per_plane = rows // planes
    plane = row // per_plane
    offset = pl.multiple_of((row % per_plane) * count, LANES)
    groups = width // LANES
    ours = lax.broadcasted_iota(jnp.int32, (planes, 1), 0) == plane
    image = jnp.sum(jnp.where(ours, est_ref[...], 0.0), axis=0, keepdims=True)
    for j in range(groups):
        table_ref[j : j + 1, :] = image[:, j * LANES : (j + 1) * LANES]
    table = table_ref[...]
    hi = table.astype(BF16)
    rest = table - hi.astype(F32)
    mid = rest.astype(BF16)
    low = (rest - mid.astype(F32)).astype(BF16)
    index = dh_ref[:, pl.ds(offset, count)]
    place = index - col * width
    group = place >> 7
    lane = place & (LANES - 1)
    one_hot = (lax.broadcasted_iota(jnp.int32, (groups, count), 0) == group).astype(F32).astype(BF16)
    found = tdot(hi, one_hot) + tdot(mid, one_hot) + tdot(low, one_hot)
    keep = lax.broadcasted_iota(jnp.int32, (LANES, count), 0) == lane
    spread(out_ref, jnp.sum(jnp.where(keep, found, 0.0), axis=0, keepdims=True))
    band, full = mask_ref.shape
    per_row = full // LANES
    pix = dh_ref[...] - row * (band * full)
    group = pix >> 7
    lane = pix & (LANES - 1)
    upper = (lax.broadcasted_iota(jnp.int32, (band * per_row, pix.shape[1]), 0) == group).astype(F32).astype(BF16)
    lower = (lax.broadcasted_iota(jnp.int32, (LANES, pix.shape[1]), 0) == lane).astype(F32).astype(BF16)
    flat_ref[...] = mm_t(upper, lower)
    for j in range(per_row):
        mask_ref[:, j * LANES : (j + 1) * LANES] = flat_ref[pl.ds(j, band, stride=per_row), :]


def gradient_kernel(field_ref, jac_ref, out_ref):
    field = gathered_sum(field_ref)
    tile_rows, width = jac_ref.shape
    tiles = width // LANES
    acc = [jnp.zeros((8, LANES), F32) for _ in range(tiles)]
    for b in range(tile_rows // LANES):
        block = jnp.broadcast_to(field[:, b * LANES : (b + 1) * LANES], (LANES, LANES)).T
        for s in range(LANES // 8):
            scale = block[s * 8 : s * 8 + 8]
            at = b * LANES + s * 8
            for l in range(tiles):
                acc[l] = acc[l] + scale * jac_ref[at : at + 8, l * LANES : (l + 1) * LANES]
    row = jnp.concatenate([jnp.sum(a, axis=0, keepdims=True) for a in acc], axis=1)
    spread(out_ref, row)


def modal_kernel(grad_ref, basis_ref, out_ref):
    grad = gathered_sum(grad_ref)
    tile_rows, width = basis_ref.shape
    tiles = width // LANES
    lanes = [jnp.broadcast_to(grad[:, l * LANES : (l + 1) * LANES], (8, LANES)) for l in range(tiles)]
    parts = []
    for b in range(tile_rows // LANES):
        pieces = []
        for s in range(LANES // 8):
            at = b * LANES + s * 8
            acc = lanes[0] * basis_ref[at : at + 8, 0:LANES]
            for l in range(1, tiles):
                acc = acc + lanes[l] * basis_ref[at : at + 8, l * LANES : (l + 1) * LANES]
            pieces.append(acc)
        parts.append(jnp.sum(jnp.concatenate(pieces, axis=0).T, axis=0, keepdims=True))
    spread(out_ref, jnp.concatenate(parts, axis=1))


def command_kernel(modal_ref, eig_ref, exp_ref, basis_ref, out_ref):
    modal = gathered_sum(modal_ref)
    cands = exp_ref.shape[0]
    tile_rows, width = basis_ref.shape
    step = 256
    cand = lax.broadcasted_iota(jnp.int32, (cands, 1), 0)
    power = jnp.zeros((cands, 1), F32)
    for k in range(cands):
        power = jnp.where(cand == k, exp_ref[k].astype(F32), power)
    damping = jnp.exp2(power)
    acc = jnp.zeros((2 * cands, width), F32)
    for b in range(tile_rows // step):
        at = slice(b * step, (b + 1) * step)
        weights = -modal[:, at] / (eig_ref[:, at] + damping)
        high = weights.astype(BF16).astype(F32)
        both = jnp.concatenate([high, weights - high], axis=0).astype(BF16)
        hi, lo = split2(basis_ref[at, :])
        acc = acc + mm(both, hi) + mm(both, lo)
    commands = acc[:cands] + acc[cands:]
    for j in range(out_ref.shape[0]):
        out_ref[j] = commands


def gather_kernel(parts_ref, out_ref, send_ref):
    total = parts_ref[0]
    for j in range(1, parts_ref.shape[0]):
        total = total + parts_ref[j]
    out_ref[...] = total
    copies = send_ref.shape[0] // total.shape[0]
    for j in range(send_ref.shape[0]):
        send_ref[j] = total[j // copies : j // copies + 1]


def check_kernel(cmd_ref, infl_ref, aber_ref, amp_ref, wave_ref, mask_ref, out_ref, stat_ref, act_ref, height_ref, hi_ref, lo_ref):
    row = lax.axis_index("rows")
    col = lax.axis_index("cols")
    waves, band, full = out_ref.shape
    pup = aber_ref.shape[0]
    blocks = cmd_ref.shape[0]
    acts = infl_ref.shape[2]
    mirrors = infl_ref.shape[0]
    groups_count = wave_ref.shape[0] // waves
    first_wave = (col % groups_count) * waves
    per_block = cmd_ref.shape[2] // acts
    per_mirror = blocks // mirrors
    surface = jnp.zeros((pup, pup), F32)
    for m in range(mirrors):
        part = jnp.concatenate([cmd_ref[m * per_mirror + j] for j in range(per_mirror)], axis=0)
        for a in range(per_block):
            act_ref[pl.ds(m * acts + a, per_mirror, stride=per_block), :acts] = part[:, a * acts : (a + 1) * acts]
        actuators = act_ref[m * acts : (m + 1) * acts, :acts]
        right = mm_t(actuators, infl_ref[m], HIGHEST)
        surface = surface + jnp.dot(infl_ref[m], right, precision=HIGHEST, preferred_element_type=F32)
    height_ref[...] = aber_ref[...] + (2.0 * STROKE) * surface
    place = (lax.broadcasted_iota(jnp.int32, (1, pup), 1).astype(F32) - (pup / 2 - 0.5)) * (1.0 / pup)
    near = lax.broadcasted_iota(jnp.int32, (8, 1), 0).astype(F32) - (full / 2 - 0.5)
    far = (lax.broadcasted_iota(jnp.int32, (full // 8, 1), 0) * 8).astype(F32)
    lane = lax.broadcasted_iota(jnp.int32, (1, LANES), 1)
    band_at = pl.multiple_of(row * band, 16)
    mask = mask_ref[...]
    stat = jnp.zeros((1, LANES), F32)
    for w in range(waves):
        inverse = 1.0 / jnp.full((1, LANES), wave_ref[first_wave + w], F32)
        inverse = jnp.concatenate([inverse] * (pup // LANES), axis=1)
        cos, sin = cos_sin_turns(height_ref[...] * inverse)
        amp = amp_ref[...]
        pupil_hi, pupil_lo = split2(jnp.concatenate([amp * cos, amp * sin], axis=1))
        turns = place * (PIXEL_SCALE * inverse)
        near_c, near_s = cos_sin_turns(near * turns)
        far_c, far_s = cos_sin_turns(far * turns)
        for g in range(full // 8):
            fc = far_c[g : g + 1]
            fs = far_s[g : g + 1]
            c = near_c * fc - near_s * fs
            s = -(near_s * fc + near_c * fs)
            rows8 = jnp.concatenate([c, s], axis=1)
            hi = rows8.astype(BF16)
            hi_ref[g * 8 : g * 8 + 8, :] = hi.astype(F32)
            lo_ref[g * 8 : g * 8 + 8, :] = rows8 - hi.astype(F32)
        y_hi = hi_ref[pl.ds(band_at, band), :].astype(BF16)
        y_lo = lo_ref[pl.ds(band_at, band), :].astype(BF16)
        y_hi = jnp.concatenate([y_hi[:, :pup], y_hi[:, pup:]], axis=0)
        y_lo = jnp.concatenate([y_lo[:, :pup], y_lo[:, pup:]], axis=0)
        up = mm(jnp.concatenate([y_hi, y_lo], axis=0), pupil_hi)
        up = up[: 2 * band] + up[2 * band :] + mm(y_hi, pupil_lo)
        mid_re = up[:band, :pup] - up[band:, pup:]
        mid_im = up[:band, pup:] + up[band:, :pup]
        mid_hi, mid_lo = split2(jnp.concatenate([mid_re, mid_im], axis=0))
        both = jnp.concatenate([mid_hi, mid_lo], axis=0)
        outs = []
        for half in range(2):
            x_hi = hi_ref[:, half * pup : (half + 1) * pup].astype(BF16)
            x_lo = lo_ref[:, half * pup : (half + 1) * pup].astype(BF16)
            o = mm_t(both, x_hi)
            outs.append(o[: 2 * band] + o[2 * band :] + mm_t(mid_hi, x_lo))
        re = outs[0][:band] - outs[1][band:]
        im = outs[1][:band] + outs[0][band:]
        intensity = re * re + im * im
        out_ref[w] = intensity
        total = jnp.sum(jnp.sum(intensity, axis=0, keepdims=True), axis=1, keepdims=True)
        hole = jnp.sum(jnp.sum(intensity * mask, axis=0, keepdims=True), axis=1, keepdims=True)
        stat = jnp.where(lane == w, total, stat)
        stat = jnp.where(lane == waves + w, hole, stat)
    spread(stat_ref, stat)


def scale_kernel(stat_ref, int_ref, out_ref, contrast_ref, *, holes):
    waves = int_ref.shape[0]
    stat = gathered_sum(stat_ref)
    scale = stat[:, :waves] / (FP * FP) + EPSILON
    contrast_ref[...] = stat[:, waves : 2 * waves] / holes / scale
    inverse = 1.0 / scale
    for w in range(waves):
        out_ref[w] = int_ref[w] * inverse[:, w : w + 1]


def call(kernel, name, outs, args, scratch=(), smem=(), mib=8):
    specs = [pl.BlockSpec(memory_space=pltpu.SMEM if i in smem else pltpu.VMEM) for i in range(len(args))]
    return pl.pallas_call(
        kernel,
        out_shape=[jax.ShapeDtypeStruct(s, F32) for s in outs],
        in_specs=specs,
        out_specs=[pl.BlockSpec(memory_space=pltpu.VMEM) for _ in outs],
        scratch_shapes=[pltpu.VMEM(s, F32) for s in scratch],
        compiler_params=pltpu.CompilerParams(vmem_limit_bytes=mib << 20),
        name=name,
    )(*args)


def exchange(x, axis):
    return lax.all_to_all(x, axis, 0, 0)


def on_device(estimate, dark_hole, jacobian, basis, eigenvalues, exponents, wavelengths, amplitude, aberration, influence):
    rows = lax.axis_size("rows")
    cols = lax.axis_size("cols")
    tile_rows, width = jacobian.shape
    modes = basis.shape[0]
    cands = exponents.shape[0]
    waves = wavelengths.shape[0] // (cols // cands)
    band = FP // rows
    holes = dark_hole.shape[0]
    groups = estimate.shape[1] // LANES
    share, mask = call(
        pick_kernel, "pick", [(cols, 1, tile_rows), (band, FP)],
        [estimate, dark_hole.reshape(1, holes)],
        scratch=[(groups, LANES), (band * FP // LANES, LANES)],
    )
    share = exchange(share, "cols")
    (grad,) = call(gradient_kernel, "gradient", [(rows, 1, width)], [share, jacobian], mib=14)
    grad = exchange(grad, "rows")
    (modal,) = call(modal_kernel, "modal", [(cols, 1, modes)], [grad, basis], mib=14)
    modal = exchange(modal, "cols")
    (parts,) = call(
        command_kernel, "commands", [(rows, cands, width)],
        [modal, eigenvalues.reshape(1, modes), exponents, basis], smem=(2,), mib=20,
    )
    parts = exchange(parts, "rows")
    commands, chosen = call(gather_kernel, "gather", [(cands, width), (cols, 1, width)], [parts])
    chosen = exchange(chosen, "cols")
    intensity, stat = call(
        check_kernel, "check", [(waves, band, FP), (rows, 1, LANES)],
        [chosen, influence, aberration, amplitude, wavelengths, mask],
        scratch=[(2 * ACT, LANES), (PUP, PUP), (FP, 2 * PUP), (FP, 2 * PUP)], smem=(4,), mib=24,
    )
    stat = exchange(stat, "rows")
    image, contrast = call(
        functools.partial(scale_kernel, holes=holes), "scale", [(waves, band, FP), (1, waves)], [stat, intensity],
    )
    return commands, image, contrast


def solution(mesh):
    return jax.shard_map(
        on_device,
        mesh=mesh,
        in_specs=(
            P(None, "cols"),
            P(),
            P("rows", "cols"),
            P("rows", "cols"),
            P("rows"),
            P(),
            P(),
            P(),
            P(),
            P(),
        ),
        out_specs=(P(None, "cols"), P("cols", "rows", None), P("cols", None)),
        check_vma=False,
    )
```

```python
import functools

import jax
import jax.numpy as jnp
from jax import lax
from jax.experimental import pallas as pl
from jax.experimental.pallas import tpu as pltpu
from jax.sharding import PartitionSpec as P

FP = 384
PUP = 256
ACT = 96
LANES = 128
EPSILON = 1e-6
STROKE = 0.05
PIXEL_SCALE = 0.25
F32 = jnp.float32
BF16 = jnp.bfloat16
HIGHEST = lax.Precision.HIGHEST

COS = (1.0, -19.73920440673828, 64.93911743164062, -85.45014190673828, 60.16762924194336, -25.967599868774414, 6.528658390045166)
SIN = (6.2831854820251465, -41.34170150756836, 81.60513305664062, -76.70301818847656, 42.02592849731445, -14.899847030639648, 3.2381374835968018)


def horner(coefs, x):
    acc = jnp.full_like(x, coefs[-1])
    for c in coefs[-2::-1]:
        acc = acc * x + c
    return acc


def cos_sin_turns(t):
    r = t - jnp.round(t)
    x = r * r
    return horner(COS, x), horner(SIN, x) * r


def split2(x):
    hi = x.astype(BF16)
    return hi, (x - hi.astype(F32)).astype(BF16)


def mm(a, b):
    return jnp.dot(a, b, preferred_element_type=F32)


def mm_t(a, b, precision=None):
    return lax.dot_general(a, b, (((1,), (1,)), ((), ())), preferred_element_type=F32, precision=precision)


def tdot(a, b):
    return lax.dot_general(a, b, (((0,), (0,)), ((), ())), preferred_element_type=F32)


def spread(ref, row):
    for j in range(ref.shape[0]):
        ref[j] = row


def gathered_sum(ref):
    total = ref[0]
    for j in range(1, ref.shape[0]):
        total = total + ref[j]
    return total


def pick_kernel(est_hbm, dh_hbm, out_ref, est_ref, dh_ref, table_ref, est_sem, dh_sem):
    row = lax.axis_index("rows")
    col = lax.axis_index("cols")
    rows = lax.axis_size("rows")
    planes, width = est_ref.shape
    count = out_ref.shape[-1]
    per_plane = rows // planes
    plane = row // per_plane
    offset = pl.multiple_of((row % per_plane) * count, LANES)
    fetch_dh = pltpu.make_async_copy(dh_hbm, dh_ref, dh_sem)
    fetch_est = pltpu.make_async_copy(est_hbm, est_ref, est_sem)
    fetch_dh.start()
    fetch_est.start()
    fetch_dh.wait()
    groups = width // LANES
    index = dh_ref[:, pl.ds(offset, count)]
    place = index - col * width
    group = place >> 7
    lane = place & (LANES - 1)
    one_hot = (lax.broadcasted_iota(jnp.int32, (groups, count), 0) == group).astype(F32).astype(BF16)
    keep = lax.broadcasted_iota(jnp.int32, (LANES, count), 0) == lane
    fetch_est.wait()
    ours = lax.broadcasted_iota(jnp.int32, (planes, 1), 0) == plane
    image = jnp.sum(jnp.where(ours, est_ref[...], 0.0), axis=0, keepdims=True)
    for j in range(groups):
        table_ref[j : j + 1, :] = image[:, j * LANES : (j + 1) * LANES]
    table = table_ref[...]
    hi = table.astype(BF16)
    rest = table - hi.astype(F32)
    mid = rest.astype(BF16)
    low = (rest - mid.astype(F32)).astype(BF16)
    found = tdot(hi, one_hot) + tdot(mid, one_hot) + tdot(low, one_hot)
    spread(out_ref, jnp.sum(jnp.where(keep, found, 0.0), axis=0, keepdims=True))


def mask_kernel(dh_ref, mask_ref, flat_ref):
    row = lax.axis_index("rows")
    band, full = mask_ref.shape
    per_row = full // LANES
    pix = dh_ref[...] - row * (band * full)
    group = pix >> 7
    lane = pix & (LANES - 1)
    upper = (lax.broadcasted_iota(jnp.int32, (band * per_row, pix.shape[1]), 0) == group).astype(F32).astype(BF16)
    lower = (lax.broadcasted_iota(jnp.int32, (LANES, pix.shape[1]), 0) == lane).astype(F32).astype(BF16)
    flat_ref[...] = mm_t(upper, lower)
    for j in range(per_row):
        mask_ref[:, j * LANES : (j + 1) * LANES] = flat_ref[pl.ds(j, band, stride=per_row), :]


def wave_inverse(wave_ref, index, width):
    inverse = 1.0 / jnp.full((1, LANES), wave_ref[index], F32)
    return jnp.concatenate([inverse] * (width // LANES), axis=1)


def first_wave(wave_ref, waves):
    return (lax.axis_index("cols") % (wave_ref.shape[0] // waves)) * waves


def table_kernel(wave_ref, hi_ref, lo_ref):
    waves, full, width = hi_ref.shape
    pup = width // 2
    start = first_wave(wave_ref, waves)
    place = (lax.broadcasted_iota(jnp.int32, (1, pup), 1).astype(F32) - (pup / 2 - 0.5)) * (1.0 / pup)
    near = lax.broadcasted_iota(jnp.int32, (8, 1), 0).astype(F32) - (full / 2 - 0.5)
    far = (lax.broadcasted_iota(jnp.int32, (full // 8, 1), 0) * 8).astype(F32)

    @pl.loop(0, waves)
    def _(w):
        turns = place * (PIXEL_SCALE * wave_inverse(wave_ref, start + w, pup))
        near_c, near_s = cos_sin_turns(near * turns)
        far_c, far_s = cos_sin_turns(far * turns)
        for g in range(0, full // 8, 2):
            rows8 = []
            for h in (g, g + 1):
                fc = far_c[h : h + 1]
                fs = far_s[h : h + 1]
                c = near_c * fc - near_s * fs
                s = near_s * fc + near_c * fs
                rows8.append(jnp.concatenate([c, -s], axis=1))
            hi, lo = split2(jnp.concatenate(rows8, axis=0))
            hi_ref[w, g * 8 : g * 8 + 16, :] = hi
            lo_ref[w, g * 8 : g * 8 + 16, :] = lo


def gradient_kernel(field_ref, jac_ref, out_ref):
    field = gathered_sum(field_ref)
    tile_rows, width = jac_ref.shape
    tiles = width // LANES
    acc = [jnp.zeros((8, LANES), F32) for _ in range(tiles)]
    for b in range(tile_rows // LANES):
        block = jnp.broadcast_to(field[:, b * LANES : (b + 1) * LANES], (LANES, LANES)).T
        for s in range(LANES // 8):
            scale = block[s * 8 : s * 8 + 8]
            at = b * LANES + s * 8
            for l in range(tiles):
                acc[l] = acc[l] + scale * jac_ref[at : at + 8, l * LANES : (l + 1) * LANES]
    row = jnp.concatenate([jnp.sum(a, axis=0, keepdims=True) for a in acc], axis=1)
    spread(out_ref, row)


def modal_kernel(grad_ref, basis_ref, out_ref):
    grad = gathered_sum(grad_ref)
    tile_rows, width = basis_ref.shape
    tiles = width // LANES
    lanes = [jnp.broadcast_to(grad[:, l * LANES : (l + 1) * LANES], (8, LANES)) for l in range(tiles)]
    parts = []
    for b in range(tile_rows // LANES):
        pieces = []
        for s in range(LANES // 8):
            at = b * LANES + s * 8
            acc = lanes[0] * basis_ref[at : at + 8, 0:LANES]
            for l in range(1, tiles):
                acc = acc + lanes[l] * basis_ref[at : at + 8, l * LANES : (l + 1) * LANES]
            pieces.append(acc)
        parts.append(jnp.sum(jnp.concatenate(pieces, axis=0).T, axis=0, keepdims=True))
    spread(out_ref, jnp.concatenate(parts, axis=1))


def command_kernel(modal_ref, eig_ref, exp_ref, basis_ref, out_ref):
    modal = gathered_sum(modal_ref)
    cands = exp_ref.shape[0]
    tile_rows, width = basis_ref.shape
    step = 256
    cand = lax.broadcasted_iota(jnp.int32, (cands, 1), 0)
    power = jnp.zeros((cands, 1), F32)
    for k in range(cands):
        power = jnp.where(cand == k, exp_ref[k].astype(F32), power)
    damping = jnp.exp2(power)
    acc = jnp.zeros((2 * cands, width), F32)
    for b in range(tile_rows // step):
        at = slice(b * step, (b + 1) * step)
        weights = -modal[:, at] / (eig_ref[:, at] + damping)
        high = weights.astype(BF16).astype(F32)
        both = jnp.concatenate([high, weights - high], axis=0).astype(BF16)
        hi, lo = split2(basis_ref[at, :])
        acc = acc + mm(both, hi) + mm(both, lo)
    commands = acc[:cands] + acc[cands:]
    for j in range(out_ref.shape[0]):
        out_ref[j] = commands


def send_kernel(parts_ref, send_ref):
    total = gathered_sum(parts_ref)
    copies = send_ref.shape[0] // total.shape[0]
    for j in range(send_ref.shape[0]):
        send_ref[j] = total[j // copies : j // copies + 1]


def total_kernel(parts_ref, out_ref):
    out_ref[...] = gathered_sum(parts_ref)


def check_kernel(cmd_ref, infl_ref, aber_ref, amp_ref, wave_ref, mask_ref, hi_ref, lo_ref, out_ref, stat_ref, act_ref, height_ref):
    row = lax.axis_index("rows")
    waves, band, full = out_ref.shape
    pup = aber_ref.shape[0]
    blocks = cmd_ref.shape[0]
    acts = infl_ref.shape[2]
    mirrors = infl_ref.shape[0]
    start = first_wave(wave_ref, waves)
    per_block = cmd_ref.shape[2] // acts
    per_mirror = blocks // mirrors
    surface = jnp.zeros((pup, pup), F32)
    for m in range(mirrors):
        part = jnp.concatenate([cmd_ref[m * per_mirror + j] for j in range(per_mirror)], axis=0)
        for a in range(per_block):
            act_ref[pl.ds(m * acts + a, per_mirror, stride=per_block), :acts] = part[:, a * acts : (a + 1) * acts]
        actuators = act_ref[m * acts : (m + 1) * acts, :acts]
        right = mm_t(actuators, infl_ref[m], HIGHEST)
        surface = surface + jnp.dot(infl_ref[m], right, precision=HIGHEST, preferred_element_type=F32)
    height_ref[...] = aber_ref[...] + (2.0 * STROKE) * surface
    lane = lax.broadcasted_iota(jnp.int32, (1, LANES), 1)
    band_at = pl.multiple_of(row * band, 16)
    mask = mask_ref[...]
    stat = jnp.zeros((1, LANES), F32)
    for w in range(waves):
        cos, sin = cos_sin_turns(height_ref[...] * wave_inverse(wave_ref, start + w, pup))
        amp = amp_ref[...]
        pupil_hi, pupil_lo = split2(jnp.concatenate([amp * cos, amp * sin], axis=1))
        y_hi = hi_ref[w, pl.ds(band_at, band), :]
        y_lo = lo_ref[w, pl.ds(band_at, band), :]
        y_hi = jnp.concatenate([y_hi[:, :pup], y_hi[:, pup:]], axis=0)
        y_lo = jnp.concatenate([y_lo[:, :pup], y_lo[:, pup:]], axis=0)
        up = mm(jnp.concatenate([y_hi, y_lo], axis=0), pupil_hi)
        up = up[: 2 * band] + up[2 * band :] + mm(y_hi, pupil_lo)
        mid_re = up[:band, :pup] - up[band:, pup:]
        mid_im = up[:band, pup:] + up[band:, :pup]
        mid_hi, mid_lo = split2(jnp.concatenate([mid_re, mid_im], axis=0))
        both = jnp.concatenate([mid_hi, mid_lo], axis=0)
        outs = []
        for half in range(2):
            o = mm_t(both, hi_ref[w, :, half * pup : (half + 1) * pup])
            outs.append(o[: 2 * band] + o[2 * band :] + mm_t(mid_hi, lo_ref[w, :, half * pup : (half + 1) * pup]))
        re = outs[0][:band] - outs[1][band:]
        im = outs[1][:band] + outs[0][band:]
        intensity = re * re + im * im
        out_ref[w] = intensity
        total = jnp.sum(jnp.sum(intensity, axis=0, keepdims=True), axis=1, keepdims=True)
        hole = jnp.sum(jnp.sum(intensity * mask, axis=0, keepdims=True), axis=1, keepdims=True)
        stat = jnp.where(lane == w, total, stat)
        stat = jnp.where(lane == waves + w, hole, stat)
    spread(stat_ref, stat)


def scale_kernel(stat_ref, int_ref, out_ref, contrast_ref, *, holes):
    waves = int_ref.shape[0]
    stat = gathered_sum(stat_ref)
    scale = stat[:, :waves] / (FP * FP) + EPSILON
    contrast_ref[...] = stat[:, waves : 2 * waves] / holes / scale
    inverse = 1.0 / scale
    for w in range(waves):
        out_ref[w] = int_ref[w] * inverse[:, w : w + 1]


def call(kernel, name, outs, args, scratch=(), smem=(), hbm=(), mib=16, cost=2e10):
    def space(i):
        return pltpu.SMEM if i in smem else pltpu.HBM if i in hbm else pltpu.VMEM

    return pl.pallas_call(
        kernel,
        out_shape=[s if isinstance(s, jax.ShapeDtypeStruct) else jax.ShapeDtypeStruct(s, F32) for s in outs],
        in_specs=[pl.BlockSpec(memory_space=space(i)) for i in range(len(args))],
        out_specs=[pl.BlockSpec(memory_space=pltpu.VMEM) for _ in outs],
        scratch_shapes=[pltpu.VMEM(s, F32) if isinstance(s, tuple) else s for s in scratch],
        compiler_params=pltpu.CompilerParams(vmem_limit_bytes=mib << 20),
        cost_estimate=pl.CostEstimate(flops=int(cost), bytes_accessed=1 << 20, transcendentals=0),
        name=name,
    )(*args)


def exchange(x, axis):
    return lax.all_to_all(x, axis, 0, 0)


def on_device(estimate, dark_hole, jacobian, basis, eigenvalues, exponents, wavelengths, amplitude, aberration, influence):
    rows = lax.axis_size("rows")
    cols = lax.axis_size("cols")
    tile_rows, width = jacobian.shape
    modes = basis.shape[0]
    cands = exponents.shape[0]
    waves = wavelengths.shape[0] // (cols // cands)
    band = FP // rows
    holes = dark_hole.shape[0]
    groups = estimate.shape[1] // LANES
    dark_hole = dark_hole.reshape(1, holes)
    (share,) = call(
        pick_kernel, "pick", [(cols, 1, tile_rows)], [estimate, dark_hole], hbm=(0, 1),
        scratch=[
            estimate.shape, pltpu.VMEM((1, holes), jnp.int32), (groups, LANES),
            pltpu.SemaphoreType.DMA, pltpu.SemaphoreType.DMA,
        ],
    )
    share = exchange(share, "cols")
    table = jax.ShapeDtypeStruct((waves, FP, 2 * PUP), BF16)
    table_hi, table_lo = call(table_kernel, "tables", [table, table], [wavelengths], smem=(0,))
    (grad,) = call(gradient_kernel, "gradient", [(rows, 1, width)], [share, jacobian])
    grad = exchange(grad, "rows")
    (mask,) = call(mask_kernel, "mask", [(band, FP)], [dark_hole], scratch=[(band * FP // LANES, LANES)])
    (modal,) = call(modal_kernel, "modal", [(cols, 1, modes)], [grad, basis])
    modal = exchange(modal, "cols")
    (parts,) = call(
        command_kernel, "commands", [(rows, cands, width)],
        [modal, eigenvalues.reshape(1, modes), exponents, basis], smem=(2,),
    )
    parts = exchange(parts, "rows")
    (chosen,) = call(send_kernel, "send", [(cols, 1, width)], [parts])
    chosen = exchange(chosen, "cols")
    (commands,) = call(total_kernel, "total", [(cands, width)], [parts])
    intensity, stat = call(
        check_kernel, "check", [(waves, band, FP), (rows, 1, LANES)],
        [chosen, influence, aberration, amplitude, wavelengths, mask, table_hi, table_lo],
        scratch=[(2 * ACT, LANES), (PUP, PUP)], smem=(4,),
    )
    stat = exchange(stat, "rows")
    image, contrast = call(
        functools.partial(scale_kernel, holes=holes), "scale", [(waves, band, FP), (1, waves)], [stat, intensity],
    )
    return commands, image, contrast


def solution(mesh):
    return jax.shard_map(
        on_device,
        mesh=mesh,
        in_specs=(
            P(None, "cols"),
            P(),
            P("rows", "cols"),
            P("rows", "cols"),
            P("rows"),
            P(),
            P(),
            P(),
            P(),
            P(),
        ),
        out_specs=(P(None, "cols"), P("cols", "rows", None), P("cols", None)),
        check_vma=False,
    )
```

```python
import functools

import jax
import jax.numpy as jnp
from jax import lax
from jax.experimental import pallas as pl
from jax.experimental.pallas import tpu as pltpu
from jax.sharding import PartitionSpec as P

FP = 384
PUP = 256
ACT = 96
LANES = 128
EPSILON = 1e-6
STROKE = 0.05
PIXEL_SCALE = 0.25
F32 = jnp.float32
BF16 = jnp.bfloat16
HIGHEST = lax.Precision.HIGHEST

COS = (1.0, -19.73920440673828, 64.93911743164062, -85.45014190673828, 60.16762924194336, -25.967599868774414, 6.528658390045166)
SIN = (6.2831854820251465, -41.34170150756836, 81.60513305664062, -76.70301818847656, 42.02592849731445, -14.899847030639648, 3.2381374835968018)


def horner(coefs, x):
    acc = jnp.full_like(x, coefs[-1])
    for c in coefs[-2::-1]:
        acc = acc * x + c
    return acc


def cos_sin_turns(t):
    r = t - jnp.round(t)
    x = r * r
    return horner(COS, x), horner(SIN, x) * r


def split2(x):
    hi = x.astype(BF16)
    return hi, (x - hi.astype(F32)).astype(BF16)


def mm(a, b):
    return jnp.dot(a, b, preferred_element_type=F32)


def mm_t(a, b, precision=None):
    return lax.dot_general(a, b, (((1,), (1,)), ((), ())), preferred_element_type=F32, precision=precision)


def tdot(a, b, precision=None):
    return lax.dot_general(a, b, (((0,), (0,)), ((), ())), preferred_element_type=F32, precision=precision)


def spread(ref, row):
    for j in range(ref.shape[0]):
        ref[j] = row


def gathered_sum(ref):
    total = ref[0]
    for j in range(1, ref.shape[0]):
        total = total + ref[j]
    return total


def pick_kernel(est_ref, dh_ref, out_ref, mask_ref, table_ref, flat_ref):
    row = lax.axis_index("rows")
    col = lax.axis_index("cols")
    rows = lax.axis_size("rows")
    planes, width = est_ref.shape
    count = out_ref.shape[-1]
    per_plane = rows // planes
    plane = row // per_plane
    offset = pl.multiple_of((row % per_plane) * count, LANES)
    groups = width // LANES
    ours = lax.broadcasted_iota(jnp.int32, (planes, 1), 0) == plane
    image = jnp.sum(jnp.where(ours, est_ref[...], 0.0), axis=0, keepdims=True)
    for j in range(groups):
        table_ref[j : j + 1, :] = image[:, j * LANES : (j + 1) * LANES]
    table = table_ref[...]
    hi = table.astype(BF16)
    rest = table - hi.astype(F32)
    mid = rest.astype(BF16)
    low = (rest - mid.astype(F32)).astype(BF16)
    index = dh_ref[:, pl.ds(offset, count)]
    place = index - col * width
    group = place >> 7
    lane = place & (LANES - 1)
    one_hot = (lax.broadcasted_iota(jnp.int32, (groups, count), 0) == group).astype(F32).astype(BF16)
    found = tdot(hi, one_hot) + tdot(mid, one_hot) + tdot(low, one_hot)
    keep = lax.broadcasted_iota(jnp.int32, (LANES, count), 0) == lane
    spread(out_ref, jnp.sum(jnp.where(keep, found, 0.0), axis=0, keepdims=True))
    band, full = mask_ref.shape
    per_row = full // LANES
    pix = dh_ref[...] - row * (band * full)
    group = pix >> 7
    lane = pix & (LANES - 1)
    upper = (lax.broadcasted_iota(jnp.int32, (band * per_row, pix.shape[1]), 0) == group).astype(F32).astype(BF16)
    lower = (lax.broadcasted_iota(jnp.int32, (LANES, pix.shape[1]), 0) == lane).astype(F32).astype(BF16)
    flat_ref[...] = mm_t(upper, lower)
    for j in range(per_row):
        mask_ref[:, j * LANES : (j + 1) * LANES] = flat_ref[pl.ds(j, band, stride=per_row), :]


def gradient_kernel(field_ref, jac_ref, out_ref):
    field = gathered_sum(field_ref)
    tile_rows, width = jac_ref.shape
    tiles = width // LANES
    acc = [jnp.zeros((8, LANES), F32) for _ in range(tiles)]
    for b in range(tile_rows // LANES):
        block = jnp.broadcast_to(field[:, b * LANES : (b + 1) * LANES], (LANES, LANES)).T
        for s in range(LANES // 8):
            scale = block[s * 8 : s * 8 + 8]
            at = b * LANES + s * 8
            for l in range(tiles):
                acc[l] = acc[l] + scale * jac_ref[at : at + 8, l * LANES : (l + 1) * LANES]
    row = jnp.concatenate([jnp.sum(a, axis=0, keepdims=True) for a in acc], axis=1)
    spread(out_ref, row)


def modal_kernel(grad_ref, basis_ref, out_ref):
    grad = gathered_sum(grad_ref)
    tile_rows, width = basis_ref.shape
    tiles = width // LANES
    lanes = [jnp.broadcast_to(grad[:, l * LANES : (l + 1) * LANES], (8, LANES)) for l in range(tiles)]
    parts = []
    for b in range(tile_rows // LANES):
        pieces = []
        for s in range(LANES // 8):
            at = b * LANES + s * 8
            acc = lanes[0] * basis_ref[at : at + 8, 0:LANES]
            for l in range(1, tiles):
                acc = acc + lanes[l] * basis_ref[at : at + 8, l * LANES : (l + 1) * LANES]
            pieces.append(acc)
        parts.append(jnp.sum(jnp.concatenate(pieces, axis=0).T, axis=0, keepdims=True))
    spread(out_ref, jnp.concatenate(parts, axis=1))


def command_kernel(modal_ref, eig_ref, exp_ref, basis_ref, out_ref):
    modal = gathered_sum(modal_ref)
    eigen = eig_ref[...].reshape(modal.shape)
    cands = exp_ref.shape[0]
    tile_rows, width = basis_ref.shape
    step = 256
    cand = lax.broadcasted_iota(jnp.int32, (cands, 1), 0)
    power = jnp.zeros((cands, 1), F32)
    for k in range(cands):
        power = jnp.where(cand == k, exp_ref[k].astype(F32), power)
    damping = jnp.exp2(power)
    acc = jnp.zeros((2 * cands, width), F32)
    for b in range(tile_rows // step):
        at = slice(b * step, (b + 1) * step)
        weights = -modal[:, at] / (eigen[:, at] + damping)
        high = weights.astype(BF16).astype(F32)
        both = jnp.concatenate([high, weights - high], axis=0).astype(BF16)
        hi, lo = split2(basis_ref[at, :])
        acc = acc + mm(both, hi) + mm(both, lo)
    commands = acc[:cands] + acc[cands:]
    for j in range(out_ref.shape[0]):
        out_ref[j] = commands


def gather_kernel(parts_ref, out_ref, send_ref):
    total = parts_ref[0]
    for j in range(1, parts_ref.shape[0]):
        total = total + parts_ref[j]
    out_ref[...] = total
    copies = send_ref.shape[0] // total.shape[0]
    for j in range(send_ref.shape[0]):
        send_ref[j] = total[j // copies : j // copies + 1]


def check_kernel(cmd_ref, infl_ref, aber_ref, amp_ref, wave_ref, mask_ref, out_ref, stat_ref, act_ref, height_ref, hi_ref, lo_ref):
    row = lax.axis_index("rows")
    col = lax.axis_index("cols")
    waves, band, full = out_ref.shape
    pup = aber_ref.shape[0]
    blocks = cmd_ref.shape[0]
    acts = infl_ref.shape[1]
    mirrors = infl_ref.shape[0]
    groups_count = wave_ref.shape[0] // waves
    first_wave = (col % groups_count) * waves
    per_block = cmd_ref.shape[2] // acts
    per_mirror = blocks // mirrors
    surface = jnp.zeros((pup, pup), F32)
    for m in range(mirrors):
        part = jnp.concatenate([cmd_ref[m * per_mirror + j] for j in range(per_mirror)], axis=0)
        for a in range(per_block):
            act_ref[pl.ds(m * acts + a, per_mirror, stride=per_block), :acts] = part[:, a * acts : (a + 1) * acts]
        actuators = act_ref[m * acts : (m + 1) * acts, :acts]
        influence = infl_ref[m]
        right = jnp.dot(actuators, influence, precision=HIGHEST, preferred_element_type=F32)
        surface = surface + tdot(influence, right, HIGHEST)
    height_ref[...] = aber_ref[...] + (2.0 * STROKE) * surface
    place = (lax.broadcasted_iota(jnp.int32, (1, pup), 1).astype(F32) - (pup / 2 - 0.5)) * (1.0 / pup)
    near = lax.broadcasted_iota(jnp.int32, (8, 1), 0).astype(F32) - (full / 2 - 0.5)
    far = (lax.broadcasted_iota(jnp.int32, (full // 8, 1), 0) * 8).astype(F32)
    lane = lax.broadcasted_iota(jnp.int32, (1, LANES), 1)
    band_at = pl.multiple_of(row * band, 16)
    mask = mask_ref[...]
    stat = jnp.zeros((1, LANES), F32)
    for w in range(waves):
        inverse = 1.0 / jnp.full((1, LANES), wave_ref[first_wave + w], F32)
        inverse = jnp.concatenate([inverse] * (pup // LANES), axis=1)
        cos, sin = cos_sin_turns(height_ref[...] * inverse)
        amp = amp_ref[...]
        pupil_hi, pupil_lo = split2(jnp.concatenate([amp * cos, amp * sin], axis=1))
        turns = place * (PIXEL_SCALE * inverse)
        near_c, near_s = cos_sin_turns(near * turns)
        far_c, far_s = cos_sin_turns(far * turns)
        for g in range(full // 8):
            fc = far_c[g : g + 1]
            fs = far_s[g : g + 1]
            c = near_c * fc - near_s * fs
            s = -(near_s * fc + near_c * fs)
            rows8 = jnp.concatenate([c, s], axis=1)
            hi = rows8.astype(BF16)
            hi_ref[g * 8 : g * 8 + 8, :] = hi.astype(F32)
            lo_ref[g * 8 : g * 8 + 8, :] = rows8 - hi.astype(F32)
        y_hi = hi_ref[pl.ds(band_at, band), :].astype(BF16)
        y_lo = lo_ref[pl.ds(band_at, band), :].astype(BF16)
        y_hi = jnp.concatenate([y_hi[:, :pup], y_hi[:, pup:]], axis=0)
        y_lo = jnp.concatenate([y_lo[:, :pup], y_lo[:, pup:]], axis=0)
        up = mm(jnp.concatenate([y_hi, y_lo], axis=0), pupil_hi)
        up = up[: 2 * band] + up[2 * band :] + mm(y_hi, pupil_lo)
        mid_re = up[:band, :pup] - up[band:, pup:]
        mid_im = up[:band, pup:] + up[band:, :pup]
        mid_hi, mid_lo = split2(jnp.concatenate([mid_re, mid_im], axis=0))
        both = jnp.concatenate([mid_hi, mid_lo], axis=0)
        outs = []
        for half in range(2):
            x_hi = hi_ref[:, half * pup : (half + 1) * pup].astype(BF16)
            x_lo = lo_ref[:, half * pup : (half + 1) * pup].astype(BF16)
            o = mm_t(both, x_hi)
            outs.append(o[: 2 * band] + o[2 * band :] + mm_t(mid_hi, x_lo))
        re = outs[0][:band] - outs[1][band:]
        im = outs[1][:band] + outs[0][band:]
        intensity = re * re + im * im
        out_ref[w] = intensity
        total = jnp.sum(jnp.sum(intensity, axis=0, keepdims=True), axis=1, keepdims=True)
        hole = jnp.sum(jnp.sum(intensity * mask, axis=0, keepdims=True), axis=1, keepdims=True)
        stat = jnp.where(lane == w, total, stat)
        stat = jnp.where(lane == waves + w, hole, stat)
    spread(stat_ref, stat)


def scale_kernel(stat_ref, int_ref, out_ref, contrast_ref, *, holes):
    waves = int_ref.shape[0]
    stat = gathered_sum(stat_ref)
    scale = stat[:, :waves] / (FP * FP) + EPSILON
    contrast_ref[...] = stat[:, waves : 2 * waves] / holes / scale
    inverse = 1.0 / scale
    for w in range(waves):
        out_ref[w] = int_ref[w] * inverse[:, w : w + 1]


def call(kernel, name, outs, args, scratch=(), smem=()):
    return pl.pallas_call(
        kernel,
        out_shape=[jax.ShapeDtypeStruct(s, F32) for s in outs],
        in_specs=[pl.BlockSpec(memory_space=pltpu.SMEM if i in smem else pltpu.VMEM) for i in range(len(args))],
        out_specs=[pl.BlockSpec(memory_space=pltpu.VMEM) for _ in outs],
        scratch_shapes=[pltpu.VMEM(s, F32) for s in scratch],
        compiler_params=pltpu.CompilerParams(vmem_limit_bytes=16 << 20),
        cost_estimate=pl.CostEstimate(flops=20_000_000_000, bytes_accessed=1 << 20, transcendentals=0),
        name=name,
    )(*args)


def exchange(x, axis):
    return lax.all_to_all(x, axis, 0, 0)


def on_device(estimate, dark_hole, jacobian, basis, eigenvalues, exponents, wavelengths, amplitude, aberration, influence):
    rows = lax.axis_size("rows")
    cols = lax.axis_size("cols")
    tile_rows, width = jacobian.shape
    modes = basis.shape[0]
    cands = exponents.shape[0]
    waves = wavelengths.shape[0] // (cols // cands)
    band = FP // rows
    holes = dark_hole.shape[0]
    groups = estimate.shape[1] // LANES
    share, mask = call(
        pick_kernel, "pick", [(cols, 1, tile_rows), (band, FP)],
        [estimate, dark_hole.reshape(1, holes)],
        scratch=[(groups, LANES), (band * FP // LANES, LANES)],
    )
    share = exchange(share, "cols")
    (grad,) = call(gradient_kernel, "gradient", [(rows, 1, width)], [share, jacobian])
    grad = exchange(grad, "rows")
    (modal,) = call(modal_kernel, "modal", [(cols, 1, modes)], [grad, basis])
    modal = exchange(modal, "cols")
    (parts,) = call(
        command_kernel, "commands", [(rows, cands, width)],
        [modal, eigenvalues, exponents, basis], smem=(2,),
    )
    parts = exchange(parts, "rows")
    commands, chosen = call(gather_kernel, "gather", [(cands, width), (cols, 1, width)], [parts])
    chosen = exchange(chosen, "cols")
    intensity, stat = call(
        check_kernel, "check", [(waves, band, FP), (rows, 1, LANES)],
        [chosen, jnp.swapaxes(influence, 1, 2), aberration, amplitude, wavelengths, mask],
        scratch=[(2 * ACT, LANES), (PUP, PUP), (FP, 2 * PUP), (FP, 2 * PUP)], smem=(4,),
    )
    stat = exchange(stat, "rows")
    image, contrast = call(
        functools.partial(scale_kernel, holes=holes), "scale", [(waves, band, FP), (1, waves)], [stat, intensity],
    )
    return commands, image, contrast


def solution(mesh):
    return jax.shard_map(
        on_device,
        mesh=mesh,
        in_specs=(
            P(None, "cols"),
            P(),
            P("rows", "cols"),
            P("rows", "cols"),
            P("rows"),
            P(),
            P(),
            P(),
            P(),
            P(),
        ),
        out_specs=(P(None, "cols"), P("cols", "rows", None), P("cols", None)),
        check_vma=False,
    )
```

```python
import functools

import jax
import jax.numpy as jnp
from jax import lax
from jax.experimental import pallas as pl
from jax.experimental.pallas import tpu as pltpu
from jax.sharding import PartitionSpec as P

FP = 384
PUP = 256
ACT = 96
LANES = 128
EPSILON = 1e-6
STROKE = 0.05
PIXEL_SCALE = 0.25
F32 = jnp.float32
BF16 = jnp.bfloat16
LEAST = -2
LEVELS = 6
HIGHEST = lax.Precision.HIGHEST

COS = (0.9999992251396179, -19.738981246948242, 64.92865753173828, -85.27162170410156, 58.79049301147461, -21.07110595703125)
SIN = (6.283185005187988, -41.341590881347656, 81.59994506835938, -76.61447143554688, 41.3428840637207, -12.471243858337402)


def horner(coefs, x):
    acc = jnp.full_like(x, coefs[-1])
    for c in coefs[-2::-1]:
        acc = acc * x + c
    return acc


def cos_sin_turns(t):
    r = t - jnp.round(t)
    x = r * r
    return horner(COS, x), horner(SIN, x) * r


def split2(x):
    hi = x.astype(BF16)
    return hi, (x - hi.astype(F32)).astype(BF16)


def mm(a, b):
    return jnp.dot(a, b, preferred_element_type=F32)


def mm_t(a, b, precision=None):
    return lax.dot_general(a, b, (((1,), (1,)), ((), ())), preferred_element_type=F32, precision=precision)


def tdot(a, b, precision=None):
    return lax.dot_general(a, b, (((0,), (0,)), ((), ())), preferred_element_type=F32, precision=precision)


def spread(ref, row):
    for j in range(ref.shape[0]):
        ref[j] = row


def gathered_sum(ref):
    total = ref[0]
    for j in range(1, ref.shape[0]):
        total = total + ref[j]
    return total


def pick_kernel(est_ref, dh_ref, out_ref, mask_ref, table_ref, flat_ref):
    row = lax.axis_index("rows")
    col = lax.axis_index("cols")
    rows = lax.axis_size("rows")
    planes, width = est_ref.shape
    count = out_ref.shape[-1]
    per_plane = rows // planes
    plane = row // per_plane
    offset = pl.multiple_of((row % per_plane) * count, LANES)
    groups = width // LANES
    ours = lax.broadcasted_iota(jnp.int32, (planes, 1), 0) == plane
    image = jnp.sum(jnp.where(ours, est_ref[...], 0.0), axis=0, keepdims=True)
    for j in range(groups):
        table_ref[j : j + 1, :] = image[:, j * LANES : (j + 1) * LANES]
    table = table_ref[...]
    hi = table.astype(BF16)
    rest = table - hi.astype(F32)
    mid = rest.astype(BF16)
    low = (rest - mid.astype(F32)).astype(BF16)
    index = dh_ref[:, pl.ds(offset, count)]
    place = index - col * width
    group = place >> 7
    lane = place & (LANES - 1)
    one_hot = (lax.broadcasted_iota(jnp.int32, (groups, count), 0) == group).astype(F32).astype(BF16)
    found = tdot(hi, one_hot) + tdot(mid, one_hot) + tdot(low, one_hot)
    keep = lax.broadcasted_iota(jnp.int32, (LANES, count), 0) == lane
    spread(out_ref, jnp.sum(jnp.where(keep, found, 0.0), axis=0, keepdims=True))
    band, full = mask_ref.shape
    per_row = full // LANES
    pix = dh_ref[...] - row * (band * full)
    group = pix >> 7
    lane = pix & (LANES - 1)
    upper = (lax.broadcasted_iota(jnp.int32, (band * per_row, pix.shape[1]), 0) == group).astype(F32).astype(BF16)
    lower = (lax.broadcasted_iota(jnp.int32, (LANES, pix.shape[1]), 0) == lane).astype(F32).astype(BF16)
    flat_ref[...] = mm_t(upper, lower)
    for j in range(per_row):
        mask_ref[:, j * LANES : (j + 1) * LANES] = flat_ref[pl.ds(j, band, stride=per_row), :]


def gradient_kernel(field_ref, jac_ref, out_ref):
    field = gathered_sum(field_ref)
    tile_rows, width = jac_ref.shape
    tiles = width // LANES
    acc = [jnp.zeros((8, LANES), F32) for _ in range(tiles)]
    for b in range(tile_rows // LANES):
        block = jnp.broadcast_to(field[:, b * LANES : (b + 1) * LANES], (LANES, LANES)).T
        for s in range(LANES // 8):
            scale = block[s * 8 : s * 8 + 8]
            at = b * LANES + s * 8
            for l in range(tiles):
                acc[l] = acc[l] + scale * jac_ref[at : at + 8, l * LANES : (l + 1) * LANES]
    row = jnp.concatenate([jnp.sum(a, axis=0, keepdims=True) for a in acc], axis=1)
    spread(out_ref, row)


def modal_kernel(grad_ref, basis_ref, out_ref):
    grad = gathered_sum(grad_ref)
    tile_rows, width = basis_ref.shape
    tiles = width // LANES
    lanes = [jnp.broadcast_to(grad[:, l * LANES : (l + 1) * LANES], (8, LANES)) for l in range(tiles)]
    parts = []
    for b in range(tile_rows // LANES):
        pieces = []
        for s in range(LANES // 8):
            at = b * LANES + s * 8
            acc = lanes[0] * basis_ref[at : at + 8, 0:LANES]
            for l in range(1, tiles):
                acc = acc + lanes[l] * basis_ref[at : at + 8, l * LANES : (l + 1) * LANES]
            pieces.append(acc)
        parts.append(jnp.sum(jnp.concatenate(pieces, axis=0).T, axis=0, keepdims=True))
    spread(out_ref, jnp.concatenate(parts, axis=1))


def command_kernel(modal_ref, eig_ref, basis_ref, out_ref):
    modal = gathered_sum(modal_ref)
    eigen = eig_ref[...].reshape(modal.shape)
    tile_rows, width = basis_ref.shape
    step = 256
    rows = 8
    damping = jnp.exp2((lax.broadcasted_iota(jnp.int32, (rows, 1), 0) + LEAST).astype(F32))
    acc = jnp.zeros((2 * rows, width), F32)
    for b in range(tile_rows // step):
        at = slice(b * step, (b + 1) * step)
        weights = -modal[:, at] / (eigen[:, at] + damping)
        high = weights.astype(BF16).astype(F32)
        both = jnp.concatenate([high, weights - high], axis=0).astype(BF16)
        hi, lo = split2(basis_ref[at, :])
        acc = acc + mm(both, hi) + mm(both, lo)
    levels = acc[:rows] + acc[rows:]
    spread(out_ref, jnp.concatenate([levels[l : l + 1] for l in range(LEVELS)], axis=1))


def gather_kernel(parts_ref, exp_ref, out_ref, send_ref, levels_ref):
    levels_ref[...] = gathered_sum(parts_ref)
    cands, width = out_ref.shape
    copies = send_ref.shape[0] // cands
    for k in range(cands):
        level = exp_ref[k] - LEAST
        row = levels_ref[:, pl.ds(pl.multiple_of(level * width, LANES), width)]
        out_ref[k : k + 1, :] = row
        for j in range(copies):
            send_ref[k * copies + j] = row


def transform(near_u, far_u, turns):
    near_c, near_s = cos_sin_turns(near_u * turns)
    far_c, far_s = cos_sin_turns(far_u * turns)
    cos = []
    sin = []
    for g in range(far_u.shape[0]):
        fc = far_c[g : g + 1]
        fs = far_s[g : g + 1]
        cos.append(near_c * fc - near_s * fs)
        sin.append(-(near_s * fc + near_c * fs))
    return jnp.concatenate([jnp.concatenate(cos, axis=0), jnp.concatenate(sin, axis=0)], axis=1)


def places(size, pup):
    return (lax.broadcasted_iota(jnp.int32, (1, size), 1).astype(F32) - (pup / 2 - 0.5)) * (1.0 / pup)


def mirror_surface(cmd_ref, infl_ref, half_refs):
    blocks = cmd_ref.shape[0]
    mirrors, acts, pup = infl_ref.shape
    per_block = cmd_ref.shape[2] // acts
    per_mirror = blocks // mirrors
    lefts = []
    for m in range(mirrors):
        halves = []
        for h in range(pup // LANES):
            half_ref = half_refs[m * (pup // LANES) + h]
            half_ref[...] = infl_ref[m, :, h * LANES : (h + 1) * LANES]
            halves.append([half_ref[pl.ds(a, per_mirror, stride=per_block), :] for a in range(per_block)])
        lefts.append(jnp.concatenate([jnp.concatenate(part, axis=0) for part in halves], axis=1))
    left_hi, left_lo = split2(jnp.concatenate(lefts, axis=0).T)
    rights = []
    for m in range(mirrors):
        part = jnp.concatenate([cmd_ref[m * per_mirror + j] for j in range(per_mirror)], axis=0)
        act_hi, act_lo = split2(jnp.concatenate([part[:, a * acts : (a + 1) * acts] for a in range(per_block)], axis=0))
        infl_hi, infl_lo = split2(infl_ref[m])
        both = mm(jnp.concatenate([act_hi, act_lo], axis=0), infl_hi)
        rights.append(both[:acts] + both[acts:] + mm(act_hi, infl_lo))
    right_hi, right_lo = split2(jnp.concatenate(rights, axis=0))
    both = mm(jnp.concatenate([left_hi, left_lo], axis=0), right_hi)
    return both[:pup] + both[pup:] + mm(left_hi, right_lo)


def turned(x):
    half = x.shape[1] // 2
    re = x[:, :half]
    im = x[:, half:]
    return jnp.concatenate([jnp.concatenate([re, -im], axis=1), jnp.concatenate([im, re], axis=1)], axis=0)


def check_scratch(waves):
    return [pltpu.SemaphoreType.DMA, pltpu.VMEM((PUP, PUP), F32)] + [pltpu.VMEM((ACT, LANES), F32)] * 4


def check_kernel(cmd_ref, infl_ref, aber_ref, amp_ref, wave_ref, mask_ref, all_ref, out_ref, stat_ref, all_out, sem, height_ref, *half_refs):
    whole = pltpu.make_async_copy(all_ref, all_out, sem)
    whole.start()
    row = lax.axis_index("rows")
    col = lax.axis_index("cols")
    waves, band, full = out_ref.shape
    pup = aber_ref.shape[0]
    half = pup // 2
    side = full // 2
    groups_count = wave_ref.shape[0] // waves
    first_wave = (col % groups_count) * waves
    lane = lax.broadcasted_iota(jnp.int32, (1, LANES), 1)
    mask = mask_ref[...]
    stat = jnp.zeros((1, LANES), F32)
    near_u = lax.broadcasted_iota(jnp.int32, (8, 1), 0).astype(F32) - (full / 2 - 0.5)
    far_u = (lax.broadcasted_iota(jnp.int32, (side // 8, 1), 0) * 8).astype(F32)
    band_u = (lax.broadcasted_iota(jnp.int32, (band // 8, 1), 0) * 8 + row * band).astype(F32)
    i = lax.broadcasted_iota(jnp.int32, (half, half), 0)
    flip = (i + lax.broadcasted_iota(jnp.int32, (half, half), 1) == half - 1).astype(F32).astype(BF16)
    i = lax.broadcasted_iota(jnp.int32, (2 * LANES, 2 * LANES), 0)
    j = lax.broadcasted_iota(jnp.int32, (2 * LANES, 2 * LANES), 1)
    back = ((i + j == full - 1 - LANES) & (i < side)).astype(F32).astype(BF16)
    inverse = []
    for w in range(waves):
        one = 1.0 / jnp.full((1, LANES), wave_ref[first_wave + w], F32)
        inverse.append(jnp.concatenate([one] * (pup // LANES), axis=1))

    def pupil(w):
        cos, sin = cos_sin_turns(height_ref[...] * inverse[w])
        amp = amp_ref[...]
        return split2(jnp.concatenate([amp * cos, amp * sin], axis=0))

    def band_table(w):
        hi, lo = split2(transform(near_u, band_u, places(pup, pup) * (PIXEL_SCALE * inverse[w])))
        return turned(hi), turned(lo)

    def half_table(w):
        return split2(transform(near_u, far_u, places(half, pup) * (PIXEL_SCALE * inverse[w][:, :half])))

    def near_side(table, held):
        pupil_hi, pupil_lo = held
        y_hi, y_lo = table
        return mm(jnp.concatenate([y_hi, y_lo], axis=0), pupil_hi), mm(y_hi, pupil_lo)

    def fold(up, low):
        up = up[: 2 * band] + up[2 * band :] + low
        upper_hi, upper_lo = split2(up[:, half:])
        return up[:, :half], mm(jnp.concatenate([upper_hi, upper_lo], axis=0), flip)

    def middle(lower, upper):
        upper = upper[: 2 * band] + upper[2 * band :]
        parts = []
        for even, odd in zip(split2(lower + upper), split2(lower - upper)):
            re = even[:band]
            im = even[band:]
            odd_re = odd[:band]
            odd_im = odd[band:]
            rows = [(re, -odd_im), (im, odd_re), (re, odd_im), (im, -odd_re)]
            rows = [jnp.concatenate(pair, axis=1) for pair in rows]
            parts.append(jnp.concatenate(rows + [jnp.zeros((2 * LANES - 4 * band, pup), BF16)], axis=0))
        return parts

    def far_side(table, mid):
        mid_hi, mid_lo = mid
        hi, lo = table
        return mm_t(hi, jnp.concatenate([mid_hi, mid_lo], axis=0)), mm_t(lo, mid_hi)

    def unfold(field, low):
        field = field[:, : 2 * LANES] + field[:, 2 * LANES :] + low
        field = jnp.concatenate([field, jnp.zeros((2 * LANES - side, 2 * LANES), F32)], axis=0).T
        field = field * field
        far_hi, far_lo = split2(field[2 * band : 3 * band] + field[3 * band : 4 * band])
        return field[:band] + field[band : 2 * band], mm(jnp.concatenate([far_hi, far_lo], axis=0), back)

    def finish(w, near, far, stat):
        far = far[:band] + far[band:]
        intensity = jnp.concatenate([near[:, :LANES], near[:, LANES:] + far[:, :LANES], far[:, LANES:]], axis=1)
        out_ref[w] = intensity
        total = jnp.sum(jnp.sum(intensity, axis=0, keepdims=True), axis=1, keepdims=True)
        hole = jnp.sum(jnp.sum(intensity * mask, axis=0, keepdims=True), axis=1, keepdims=True)
        stat = jnp.where(lane == w, total, stat)
        return jnp.where(lane == waves + w, hole, stat)

    height_ref[...] = aber_ref[...] + (2.0 * STROKE) * mirror_surface(cmd_ref, infl_ref, half_refs)
    first, folded, mid, field, image = {}, {}, {}, {}, {}
    for step in range(waves + 4):
        if step < waves:
            first[step] = near_side(band_table(step), pupil(step))
        w = step - 1
        if 0 <= w < waves:
            folded[w] = fold(*first.pop(w))
        w = step - 2
        if 0 <= w < waves:
            field[w] = far_side(half_table(w), middle(*folded.pop(w)))
        w = step - 3
        if 0 <= w < waves:
            image[w] = unfold(*field.pop(w))
        w = step - 4
        if 0 <= w < waves:
            stat = finish(w, *image.pop(w), stat)
    spread(stat_ref, stat)
    whole.wait()


def scale_kernel(stat_ref, int_ref, out_ref, contrast_ref, *, holes):
    waves = int_ref.shape[0]
    stat = gathered_sum(stat_ref)
    scale = stat[:, :waves] / (FP * FP) + EPSILON
    contrast_ref[...] = stat[:, waves : 2 * waves] / holes / scale
    inverse = 1.0 / scale
    for w in range(waves):
        out_ref[w] = int_ref[w] * inverse[:, w : w + 1]


def call(kernel, name, outs, args, scratch=(), smem=(), hbm_out=()):
    return pl.pallas_call(
        kernel,
        out_shape=[jax.ShapeDtypeStruct(s, F32) for s in outs],
        in_specs=[pl.BlockSpec(memory_space=pltpu.SMEM if i in smem else pltpu.VMEM) for i in range(len(args))],
        out_specs=[pl.BlockSpec(memory_space=pl.ANY if i in hbm_out else pltpu.VMEM) for i in range(len(outs))],
        scratch_shapes=[pltpu.VMEM(s, F32) if isinstance(s, tuple) else s for s in scratch],
        compiler_params=pltpu.CompilerParams(vmem_limit_bytes=16 << 20),
        cost_estimate=pl.CostEstimate(flops=20_000_000_000, bytes_accessed=1 << 20, transcendentals=0),
        name=name,
    )(*args)


def exchange(x, axis):
    return lax.all_to_all(x, axis, 0, 0)


def on_device(estimate, dark_hole, jacobian, basis, eigenvalues, exponents, wavelengths, amplitude, aberration, influence):
    rows = lax.axis_size("rows")
    cols = lax.axis_size("cols")
    tile_rows, width = jacobian.shape
    modes = basis.shape[0]
    cands = exponents.shape[0]
    waves = wavelengths.shape[0] // (cols // cands)
    band = FP // rows
    holes = dark_hole.shape[0]
    groups = estimate.shape[1] // LANES
    share, mask = call(
        pick_kernel, "pick", [(cols, 1, tile_rows), (band, FP)],
        [estimate, dark_hole.reshape(1, holes)],
        scratch=[(groups, LANES), (band * FP // LANES, LANES)],
    )
    share = exchange(share, "cols")
    (grad,) = call(gradient_kernel, "gradient", [(rows, 1, width)], [share, jacobian])
    grad = exchange(grad, "rows")
    (modal,) = call(modal_kernel, "modal", [(cols, 1, modes)], [grad, basis])
    modal = exchange(modal, "cols")
    (parts,) = call(command_kernel, "commands", [(rows, 1, LEVELS * width)], [modal, eigenvalues, basis])
    parts = exchange(parts, "rows")
    commands, chosen = call(
        gather_kernel, "gather", [(cands, width), (cols, 1, width)], [parts, exponents],
        scratch=[(1, LEVELS * width)], smem=(1,),
    )
    chosen = exchange(chosen, "cols")
    intensity, stat, commands = call(
        check_kernel, "check", [(waves, band, FP), (rows, 1, LANES), (cands, width)],
        [chosen, jnp.swapaxes(influence, 1, 2), aberration, amplitude, wavelengths, mask, commands],
        scratch=check_scratch(waves), smem=(4,), hbm_out=(2,),
    )
    stat = exchange(stat, "rows")
    image, contrast = call(
        functools.partial(scale_kernel, holes=holes), "scale", [(waves, band, FP), (1, waves)], [stat, intensity],
    )
    return commands, image, contrast


def solution(mesh):
    return jax.shard_map(
        on_device,
        mesh=mesh,
        in_specs=(
            P(None, "cols"),
            P(),
            P("rows", "cols"),
            P("rows", "cols"),
            P("rows"),
            P(),
            P(),
            P(),
            P(),
            P(),
        ),
        out_specs=(P(None, "cols"), P("cols", "rows", None), P("cols", None)),
        check_vma=False,
    )
```

```python
import functools

import jax
import jax.numpy as jnp
from jax import lax
from jax.experimental import pallas as pl
from jax.experimental.pallas import tpu as pltpu
from jax.sharding import PartitionSpec as P

FP = 384
PUP = 256
ACT = 96
LANES = 128
EPSILON = 1e-6
STROKE = 0.05
PIXEL_SCALE = 0.25
F32 = jnp.float32
BF16 = jnp.bfloat16
LEAST = -2
LEVELS = 6
HIGHEST = lax.Precision.HIGHEST

COS = (0.9999992251396179, -19.738981246948242, 64.92865753173828, -85.27162170410156, 58.79049301147461, -21.07110595703125)
SIN = (6.283185005187988, -41.341590881347656, 81.59994506835938, -76.61447143554688, 41.3428840637207, -12.471243858337402)


def horner(coefs, x):
    acc = jnp.full_like(x, coefs[-1])
    for c in coefs[-2::-1]:
        acc = acc * x + c
    return acc


def cos_sin_turns(t):
    r = t - jnp.round(t)
    x = r * r
    return horner(COS, x), horner(SIN, x) * r


def split2(x):
    hi = x.astype(BF16)
    return hi, (x - hi.astype(F32)).astype(BF16)


def mm(a, b):
    return jnp.dot(a, b, preferred_element_type=F32)


def mm_t(a, b, precision=None):
    return lax.dot_general(a, b, (((1,), (1,)), ((), ())), preferred_element_type=F32, precision=precision)


def tdot(a, b, precision=None):
    return lax.dot_general(a, b, (((0,), (0,)), ((), ())), preferred_element_type=F32, precision=precision)


def spread(ref, row):
    for j in range(ref.shape[0]):
        ref[j] = row


def gathered_sum(ref):
    total = ref[0]
    for j in range(1, ref.shape[0]):
        total = total + ref[j]
    return total


def reversal_kernel(flip_ref, back_ref):
    half = flip_ref.shape[0]
    wide = back_ref.shape[0]
    i = lax.broadcasted_iota(jnp.int32, (half, half), 0)
    j = lax.broadcasted_iota(jnp.int32, (half, half), 1)
    flip_ref[...] = (i + j == half - 1).astype(F32).astype(BF16)
    i = lax.broadcasted_iota(jnp.int32, (wide, wide), 0)
    j = lax.broadcasted_iota(jnp.int32, (wide, wide), 1)
    back_ref[...] = ((i + j == FP - 1 - (FP - wide)) & (i < FP // 2)).astype(F32).astype(BF16)


def one_hot(rows, index):
    held = jnp.clip(index, -1, 255).astype(F32).astype(BF16)
    row = lax.broadcasted_iota(jnp.int32, (rows, 1), 0).astype(F32).astype(BF16)
    return jnp.where(row == held, jnp.ones((), BF16), jnp.zeros((), BF16))


def pick_kernel(est_ref, dh_ref, after_ref, out_ref, mask_ref, plane_ref, flat_ref):
    row = lax.axis_index("rows")
    col = lax.axis_index("cols")
    planes, width = est_ref.shape
    groups = width // LANES
    count = out_ref.shape[-1]
    per_plane = lax.axis_size("rows") // planes
    offset = pl.multiple_of((row % per_plane) * count, LANES)
    ours = lax.broadcasted_iota(jnp.int32, (planes, 1), 0) == row // per_plane
    plane = jnp.sum(jnp.where(ours, est_ref[...], 0.0), axis=0, keepdims=True)
    for j in range(groups):
        plane_ref[j : j + 1, :] = plane[:, j * LANES : (j + 1) * LANES]
    hi, lo = split2(plane_ref[...])
    place = dh_ref[:, pl.ds(offset, count)] - col * (groups * LANES)
    chosen = one_hot(groups, place >> 7)
    found = tdot(hi, chosen) + tdot(lo, chosen)
    keep = lax.broadcasted_iota(jnp.int32, (LANES, count), 0) == (place & (LANES - 1))
    spread(out_ref, jnp.sum(jnp.where(keep, found, 0.0), axis=0, keepdims=True))
    band, full = mask_ref.shape
    per_row = full // LANES
    pix = dh_ref[...] - row * (band * full)
    flat_ref[...] = mm_t(one_hot(band * per_row, pix >> 7), one_hot(LANES, pix & (LANES - 1)))
    for j in range(per_row):
        mask_ref[:, j * LANES : (j + 1) * LANES] = flat_ref[pl.ds(j, band, stride=per_row), :]


def gradient_kernel(field_ref, jac_ref, out_ref):
    field = gathered_sum(field_ref)
    tile_rows, width = jac_ref.shape
    tiles = width // LANES
    acc = [jnp.zeros((8, LANES), F32) for _ in range(tiles)]
    for b in range(tile_rows // LANES):
        block = jnp.broadcast_to(field[:, b * LANES : (b + 1) * LANES], (LANES, LANES)).T
        for s in range(LANES // 8):
            scale = block[s * 8 : s * 8 + 8]
            at = b * LANES + s * 8
            for l in range(tiles):
                acc[l] = acc[l] + scale * jac_ref[at : at + 8, l * LANES : (l + 1) * LANES]
    row = jnp.concatenate([jnp.sum(a, axis=0, keepdims=True) for a in acc], axis=1)
    spread(out_ref, row)


def modal_kernel(grad_ref, basis_ref, out_ref):
    grad = gathered_sum(grad_ref)
    tile_rows, width = basis_ref.shape
    tiles = width // LANES
    lanes = [jnp.broadcast_to(grad[:, l * LANES : (l + 1) * LANES], (8, LANES)) for l in range(tiles)]
    parts = []
    for b in range(tile_rows // LANES):
        pieces = []
        for s in range(LANES // 8):
            at = b * LANES + s * 8
            acc = lanes[0] * basis_ref[at : at + 8, 0:LANES]
            for l in range(1, tiles):
                acc = acc + lanes[l] * basis_ref[at : at + 8, l * LANES : (l + 1) * LANES]
            pieces.append(acc)
        parts.append(jnp.sum(jnp.concatenate(pieces, axis=0).T, axis=0, keepdims=True))
    spread(out_ref, jnp.concatenate(parts, axis=1))


def command_kernel(modal_ref, eig_ref, basis_ref, out_ref):
    modal = gathered_sum(modal_ref)
    eigen = eig_ref[...].reshape(modal.shape)
    tile_rows, width = basis_ref.shape
    step = 256
    rows = 8
    damping = jnp.exp2((lax.broadcasted_iota(jnp.int32, (rows, 1), 0) + LEAST).astype(F32))
    acc = jnp.zeros((2 * rows, width), F32)
    for b in range(tile_rows // step):
        at = slice(b * step, (b + 1) * step)
        weights = -modal[:, at] / (eigen[:, at] + damping)
        high = weights.astype(BF16).astype(F32)
        both = jnp.concatenate([high, weights - high], axis=0).astype(BF16)
        hi, lo = split2(basis_ref[at, :])
        acc = acc + mm(both, hi) + mm(both, lo)
    levels = acc[:rows] + acc[rows:]
    spread(out_ref, jnp.concatenate([levels[l : l + 1] for l in range(LEVELS)], axis=1))


def gather_kernel(parts_ref, exp_ref, out_ref, send_ref, levels_ref):
    levels_ref[...] = gathered_sum(parts_ref)
    cands, width = out_ref.shape
    copies = send_ref.shape[0] // cands
    for k in range(cands):
        level = exp_ref[k] - LEAST
        row = levels_ref[:, pl.ds(pl.multiple_of(level * width, LANES), width)]
        out_ref[k : k + 1, :] = row
        for j in range(copies):
            send_ref[k * copies + j] = row


def transform(near_u, far_u, turns):
    near_c, near_s = cos_sin_turns(near_u * turns)
    far_c, far_s = cos_sin_turns(far_u * turns)
    cos = []
    sin = []
    for g in range(far_u.shape[0]):
        fc = far_c[g : g + 1]
        fs = far_s[g : g + 1]
        cos.append(near_c * fc - near_s * fs)
        sin.append(-(near_s * fc + near_c * fs))
    return jnp.concatenate([jnp.concatenate(cos, axis=0), jnp.concatenate(sin, axis=0)], axis=1)


def places(size, pup):
    return (lax.broadcasted_iota(jnp.int32, (1, size), 1).astype(F32) - (pup / 2 - 0.5)) * (1.0 / pup)


def mirror_surface(cmd_ref, infl_ref, half_refs):
    blocks = cmd_ref.shape[0]
    mirrors, acts, pup = infl_ref.shape
    per_block = cmd_ref.shape[2] // acts
    per_mirror = blocks // mirrors
    lefts = []
    for m in range(mirrors):
        halves = []
        for h in range(pup // LANES):
            half_ref = half_refs[m * (pup // LANES) + h]
            half_ref[...] = infl_ref[m, :, h * LANES : (h + 1) * LANES]
            halves.append([half_ref[pl.ds(a, per_mirror, stride=per_block), :] for a in range(per_block)])
        lefts.append(jnp.concatenate([jnp.concatenate(part, axis=0) for part in halves], axis=1))
    left_hi, left_lo = split2(jnp.concatenate(lefts, axis=0).T)
    rights = []
    for m in range(mirrors):
        part = jnp.concatenate([cmd_ref[m * per_mirror + j] for j in range(per_mirror)], axis=0)
        act_hi, act_lo = split2(jnp.concatenate([part[:, a * acts : (a + 1) * acts] for a in range(per_block)], axis=0))
        infl_hi, infl_lo = split2(infl_ref[m])
        both = mm(jnp.concatenate([act_hi, act_lo], axis=0), infl_hi)
        rights.append(both[:acts] + both[acts:] + mm(act_hi, infl_lo))
    right_hi, right_lo = split2(jnp.concatenate(rights, axis=0))
    both = mm(jnp.concatenate([left_hi, left_lo], axis=0), right_hi)
    return both[:pup] + both[pup:] + mm(left_hi, right_lo)


def turned(x):
    half = x.shape[1] // 2
    re = x[:, :half]
    im = x[:, half:]
    return jnp.concatenate([jnp.concatenate([re, -im], axis=1), jnp.concatenate([im, re], axis=1)], axis=0)


def check_scratch(waves):
    return [pltpu.SemaphoreType.DMA, pltpu.VMEM((PUP, PUP), F32)] + [pltpu.VMEM((ACT, LANES), F32)] * 4


def check_kernel(cmd_ref, infl_ref, aber_ref, amp_ref, wave_ref, mask_ref, all_ref, flip_ref, back_ref, out_ref, stat_ref, all_out, sem, height_ref, *half_refs):
    whole = pltpu.make_async_copy(all_ref, all_out, sem)
    whole.start()
    row = lax.axis_index("rows")
    col = lax.axis_index("cols")
    waves, band, full = out_ref.shape
    pup = aber_ref.shape[0]
    half = pup // 2
    side = full // 2
    groups_count = wave_ref.shape[0] // waves
    first_wave = (col % groups_count) * waves
    lane = lax.broadcasted_iota(jnp.int32, (1, LANES), 1)
    mask = mask_ref[...]
    stat = jnp.zeros((1, LANES), F32)
    near_u = lax.broadcasted_iota(jnp.int32, (8, 1), 0).astype(F32) - (full / 2 - 0.5)
    far_u = (lax.broadcasted_iota(jnp.int32, (side // 8, 1), 0) * 8).astype(F32)
    band_u = (lax.broadcasted_iota(jnp.int32, (band // 8, 1), 0) * 8 + row * band).astype(F32)
    flip = flip_ref[...]
    back = back_ref[...]
    inverse = []
    for w in range(waves):
        one = 1.0 / jnp.full((1, LANES), wave_ref[first_wave + w], F32)
        inverse.append(jnp.concatenate([one] * (pup // LANES), axis=1))

    def pupil(w):
        cos, sin = cos_sin_turns(height_ref[...] * inverse[w])
        amp = amp_ref[...]
        return split2(jnp.concatenate([amp * cos, amp * sin], axis=0))

    def band_table(w):
        hi, lo = split2(transform(near_u, band_u, places(pup, pup) * (PIXEL_SCALE * inverse[w])))
        return turned(hi), turned(lo)

    def half_table(w):
        return split2(transform(near_u, far_u, places(half, pup) * (PIXEL_SCALE * inverse[w][:, :half])))

    def near_side(table, held):
        pupil_hi, pupil_lo = held
        y_hi, y_lo = table
        return mm(jnp.concatenate([y_hi, y_lo], axis=0), pupil_hi), mm(y_hi, pupil_lo)

    def fold(up, low):
        up = up[: 2 * band] + up[2 * band :] + low
        upper_hi, upper_lo = split2(up[:, half:])
        return up[:, :half], mm(jnp.concatenate([upper_hi, upper_lo], axis=0), flip)

    def middle(lower, upper):
        upper = upper[: 2 * band] + upper[2 * band :]
        parts = []
        for even, odd in zip(split2(lower + upper), split2(lower - upper)):
            re = even[:band]
            im = even[band:]
            odd_re = odd[:band]
            odd_im = odd[band:]
            rows = [(re, -odd_im), (im, odd_re), (re, odd_im), (im, -odd_re)]
            rows = [jnp.concatenate(pair, axis=1) for pair in rows]
            parts.append(jnp.concatenate(rows + [jnp.zeros((2 * LANES - 4 * band, pup), BF16)], axis=0))
        return parts

    def far_side(table, mid):
        mid_hi, mid_lo = mid
        hi, lo = table
        return mm_t(hi, jnp.concatenate([mid_hi, mid_lo], axis=0)), mm_t(lo, mid_hi)

    def unfold(field, low):
        field = field[:, : 2 * LANES] + field[:, 2 * LANES :] + low
        field = jnp.concatenate([field, jnp.zeros((2 * LANES - side, 2 * LANES), F32)], axis=0).T
        field = field * field
        far_hi, far_lo = split2(field[2 * band : 3 * band] + field[3 * band : 4 * band])
        return field[:band] + field[band : 2 * band], mm(jnp.concatenate([far_hi, far_lo], axis=0), back)

    def finish(w, near, far, stat):
        far = far[:band] + far[band:]
        intensity = jnp.concatenate([near[:, :LANES], near[:, LANES:] + far[:, :LANES], far[:, LANES:]], axis=1)
        out_ref[w] = intensity
        total = jnp.sum(jnp.sum(intensity, axis=0, keepdims=True), axis=1, keepdims=True)
        hole = jnp.sum(jnp.sum(intensity * mask, axis=0, keepdims=True), axis=1, keepdims=True)
        stat = jnp.where(lane == w, total, stat)
        return jnp.where(lane == waves + w, hole, stat)

    height_ref[...] = aber_ref[...] + (2.0 * STROKE) * mirror_surface(cmd_ref, infl_ref, half_refs)
    first, folded, mid, field, image = {}, {}, {}, {}, {}
    for step in range(waves + 4):
        if step < waves:
            first[step] = near_side(band_table(step), pupil(step))
        w = step - 1
        if 0 <= w < waves:
            folded[w] = fold(*first.pop(w))
        w = step - 2
        if 0 <= w < waves:
            field[w] = far_side(half_table(w), middle(*folded.pop(w)))
        w = step - 3
        if 0 <= w < waves:
            image[w] = unfold(*field.pop(w))
        w = step - 4
        if 0 <= w < waves:
            stat = finish(w, *image.pop(w), stat)
    spread(stat_ref, stat)
    whole.wait()


def scale_kernel(stat_ref, int_ref, out_ref, contrast_ref, *, holes):
    waves = int_ref.shape[0]
    stat = gathered_sum(stat_ref)
    scale = stat[:, :waves] / (FP * FP) + EPSILON
    contrast_ref[...] = stat[:, waves : 2 * waves] / holes / scale
    inverse = 1.0 / scale
    for w in range(waves):
        out_ref[w] = int_ref[w] * inverse[:, w : w + 1]


def call(kernel, name, outs, args, scratch=(), smem=(), hbm=(), hbm_out=()):
    def space(i):
        return pltpu.SMEM if i in smem else pl.ANY if i in hbm else pltpu.VMEM

    return pl.pallas_call(
        kernel,
        out_shape=[jax.ShapeDtypeStruct(s, F32) if isinstance(s, tuple) else s for s in outs],
        in_specs=[pl.BlockSpec(memory_space=space(i)) for i in range(len(args))],
        out_specs=[pl.BlockSpec(memory_space=pl.ANY if i in hbm_out else pltpu.VMEM) for i in range(len(outs))],
        scratch_shapes=[pltpu.VMEM(s, F32) if isinstance(s, tuple) else s for s in scratch],
        compiler_params=pltpu.CompilerParams(vmem_limit_bytes=16 << 20),
        cost_estimate=pl.CostEstimate(flops=20_000_000_000, bytes_accessed=1 << 20, transcendentals=0),
        name=name,
    )(*args)


def exchange(x, axis):
    return lax.all_to_all(x, axis, 0, 0)


def on_device(estimate, dark_hole, jacobian, basis, eigenvalues, exponents, wavelengths, amplitude, aberration, influence):
    rows = lax.axis_size("rows")
    cols = lax.axis_size("cols")
    tile_rows, width = jacobian.shape
    modes = basis.shape[0]
    cands = exponents.shape[0]
    waves = wavelengths.shape[0] // (cols // cands)
    band = FP // rows
    holes = dark_hole.shape[0]
    square = [jax.ShapeDtypeStruct((n, n), BF16) for n in (PUP // 2, 2 * LANES)]
    flip, back = call(reversal_kernel, "reversals", square, [])
    share, mask = call(
        pick_kernel, "pick", [(cols, 1, tile_rows), (band, FP)],
        [estimate, dark_hole.reshape(1, holes), flip],
        scratch=[(estimate.shape[1] // LANES, LANES), (band * FP // LANES, LANES)], hbm=(2,),
    )
    share = exchange(share, "cols")
    (grad,) = call(gradient_kernel, "gradient", [(rows, 1, width)], [share, jacobian])
    grad = exchange(grad, "rows")
    (modal,) = call(modal_kernel, "modal", [(cols, 1, modes)], [grad, basis])
    modal = exchange(modal, "cols")
    (parts,) = call(command_kernel, "commands", [(rows, 1, LEVELS * width)], [modal, eigenvalues, basis])
    parts = exchange(parts, "rows")
    commands, chosen = call(
        gather_kernel, "gather", [(cands, width), (cols, 1, width)], [parts, exponents],
        scratch=[(1, LEVELS * width)], smem=(1,),
    )
    chosen = exchange(chosen, "cols")
    intensity, stat, commands = call(
        check_kernel, "check", [(waves, band, FP), (rows, 1, LANES), (cands, width)],
        [chosen, jnp.swapaxes(influence, 1, 2), aberration, amplitude, wavelengths, mask, commands, flip, back],
        scratch=check_scratch(waves), smem=(4,), hbm_out=(2,),
    )
    stat = exchange(stat, "rows")
    image, contrast = call(
        functools.partial(scale_kernel, holes=holes), "scale", [(waves, band, FP), (1, waves)], [stat, intensity],
    )
    return commands, image, contrast


def solution(mesh):
    return jax.shard_map(
        on_device,
        mesh=mesh,
        in_specs=(
            P(None, "cols"),
            P(),
            P("rows", "cols"),
            P("rows", "cols"),
            P("rows"),
            P(),
            P(),
            P(),
            P(),
            P(),
        ),
        out_specs=(P(None, "cols"), P("cols", "rows", None), P("cols", None)),
        check_vma=False,
    )
```

```python
import functools

import jax
import jax.numpy as jnp
from jax import lax
from jax.experimental import pallas as pl
from jax.experimental.pallas import tpu as pltpu
from jax.sharding import PartitionSpec as P

FP = 384
PUP = 256
ACT = 96
LANES = 128
EPSILON = 1e-6
STROKE = 0.05
PIXEL_SCALE = 0.25
F32 = jnp.float32
BF16 = jnp.bfloat16
LEAST = -2
LEVELS = 6
HIGHEST = lax.Precision.HIGHEST

COS = (0.9999992251396179, -19.738981246948242, 64.92865753173828, -85.27162170410156, 58.79049301147461, -21.07110595703125)
SIN = (6.283185005187988, -41.341590881347656, 81.59994506835938, -76.61447143554688, 41.3428840637207, -12.471243858337402)


def horner(coefs, x):
    acc = jnp.full_like(x, coefs[-1])
    for c in coefs[-2::-1]:
        acc = acc * x + c
    return acc


def cos_sin_turns(t):
    r = t - jnp.round(t)
    x = r * r
    return horner(COS, x), horner(SIN, x) * r


def split2(x):
    hi = x.astype(BF16)
    return hi, (x - hi.astype(F32)).astype(BF16)


def mm(a, b):
    return jnp.dot(a, b, preferred_element_type=F32)


def mm_t(a, b, precision=None):
    return lax.dot_general(a, b, (((1,), (1,)), ((), ())), preferred_element_type=F32, precision=precision)


def tdot(a, b, precision=None):
    return lax.dot_general(a, b, (((0,), (0,)), ((), ())), preferred_element_type=F32, precision=precision)


def spread(ref, row):
    for j in range(ref.shape[0]):
        ref[j] = row


def spread_rows(ref, row):
    for b in range(ref.shape[1]):
        ref[0, b : b + 1, :] = row[:, b * LANES : (b + 1) * LANES]
    block = ref[0]
    for j in range(1, ref.shape[0]):
        ref[j] = block


def gathered_sum(ref):
    total = ref[0]
    for j in range(1, ref.shape[0]):
        total = total + ref[j]
    return total


def reversal_kernel(flip_ref, back_ref):
    half = flip_ref.shape[0]
    side, wide = back_ref.shape
    i = lax.broadcasted_iota(jnp.int32, (half, half), 0)
    j = lax.broadcasted_iota(jnp.int32, (half, half), 1)
    flip_ref[...] = (i + j == half - 1).astype(F32).astype(BF16)
    i = lax.broadcasted_iota(jnp.int32, (side, wide), 0)
    j = lax.broadcasted_iota(jnp.int32, (side, wide), 1)
    back_ref[...] = (i + j == wide - 1).astype(F32).astype(BF16)


def one_hot(rows, index):
    held = jnp.clip(index, -1, 255).astype(F32).astype(BF16)
    row = lax.broadcasted_iota(jnp.int32, (rows, 1), 0).astype(F32).astype(BF16)
    return jnp.where(row == held, jnp.ones((), BF16), jnp.zeros((), BF16))


def pick_kernel(est_ref, dh_ref, after_ref, out_ref, mask_ref, plane_ref, flat_ref):
    row = lax.axis_index("rows")
    col = lax.axis_index("cols")
    planes, width = est_ref.shape
    groups = width // LANES
    count = out_ref.shape[-1]
    per_plane = lax.axis_size("rows") // planes
    offset = pl.multiple_of((row % per_plane) * count, LANES)
    ours = lax.broadcasted_iota(jnp.int32, (planes, 1), 0) == row // per_plane
    plane = jnp.sum(jnp.where(ours, est_ref[...], 0.0), axis=0, keepdims=True)
    for j in range(groups):
        plane_ref[j : j + 1, :] = plane[:, j * LANES : (j + 1) * LANES]
    hi, lo = split2(plane_ref[...])
    place = dh_ref[:, pl.ds(offset, count)] - col * (groups * LANES)
    chosen = one_hot(groups, place >> 7)
    found = tdot(hi, chosen) + tdot(lo, chosen)
    keep = lax.broadcasted_iota(jnp.int32, (LANES, count), 0) == (place & (LANES - 1))
    spread(out_ref, jnp.sum(jnp.where(keep, found, 0.0), axis=0, keepdims=True))
    band, full = mask_ref.shape
    per_row = full // LANES
    pix = dh_ref[...] - row * (band * full)
    flat_ref[...] = mm_t(one_hot(band * per_row, pix >> 7), one_hot(LANES, pix & (LANES - 1)))
    for j in range(per_row):
        mask_ref[:, j * LANES : (j + 1) * LANES] = flat_ref[pl.ds(j, band, stride=per_row), :]


def gradient_kernel(field_ref, jac_ref, out_ref):
    field = gathered_sum(field_ref)
    tile_rows, width = jac_ref.shape
    tiles = width // LANES
    acc = [jnp.zeros((8, LANES), F32) for _ in range(tiles)]
    for b in range(tile_rows // LANES):
        block = jnp.broadcast_to(field[:, b * LANES : (b + 1) * LANES], (LANES, LANES)).T
        for s in range(LANES // 8):
            scale = block[s * 8 : s * 8 + 8]
            at = b * LANES + s * 8
            for l in range(tiles):
                acc[l] = acc[l] + scale * jac_ref[at : at + 8, l * LANES : (l + 1) * LANES]
    row = jnp.concatenate([jnp.sum(a, axis=0, keepdims=True) for a in acc], axis=1)
    spread(out_ref, row)


def modal_kernel(grad_ref, basis_ref, out_ref):
    grad = gathered_sum(grad_ref)
    tile_rows, width = basis_ref.shape
    tiles = width // LANES
    lanes = [jnp.broadcast_to(grad[:, l * LANES : (l + 1) * LANES], (8, LANES)) for l in range(tiles)]
    parts = []
    for b in range(tile_rows // LANES):
        pieces = []
        for s in range(LANES // 8):
            at = b * LANES + s * 8
            acc = lanes[0] * basis_ref[at : at + 8, 0:LANES]
            for l in range(1, tiles):
                acc = acc + lanes[l] * basis_ref[at : at + 8, l * LANES : (l + 1) * LANES]
            pieces.append(acc)
        parts.append(jnp.sum(jnp.concatenate(pieces, axis=0).T, axis=0, keepdims=True))
    spread(out_ref, jnp.concatenate(parts, axis=1))


def command_kernel(modal_ref, eig_ref, basis_ref, out_ref):
    modal = gathered_sum(modal_ref)
    eigen = eig_ref[...].reshape(modal.shape)
    tile_rows, width = basis_ref.shape
    step = 256
    rows = 8
    damping = jnp.exp2((lax.broadcasted_iota(jnp.int32, (rows, 1), 0) + LEAST).astype(F32))
    acc = jnp.zeros((2 * rows, width), F32)
    for b in range(tile_rows // step):
        at = slice(b * step, (b + 1) * step)
        weights = -modal[:, at] / (eigen[:, at] + damping)
        high = weights.astype(BF16).astype(F32)
        both = jnp.concatenate([high, weights - high], axis=0).astype(BF16)
        hi, lo = split2(basis_ref[at, :])
        acc = acc + mm(both, hi) + mm(both, lo)
    levels = acc[:rows] + acc[rows:]
    spread_rows(out_ref, jnp.concatenate([levels[l : l + 1] for l in range(LEVELS)], axis=1))


def gather_kernel(parts_ref, exp_ref, out_ref, send_ref, levels_ref):
    total = gathered_sum(parts_ref)
    for b in range(levels_ref.shape[0]):
        levels_ref[b] = total[b : b + 1]
    cands, width = out_ref.shape
    copies = send_ref.shape[0] // cands
    tiles = width // LANES
    for k in range(cands):
        start = (exp_ref[k] - LEAST) * tiles
        for t in range(tiles):
            piece = levels_ref[start + t]
            at = slice(t * LANES, (t + 1) * LANES)
            out_ref[k : k + 1, at] = piece
            for j in range(copies):
                send_ref[k * copies + j, :, at] = piece


def transform(near_u, far_u, turns):
    near_c, near_s = cos_sin_turns(near_u * turns)
    far_c, far_s = cos_sin_turns(far_u * turns)
    cos = []
    sin = []
    for g in range(far_u.shape[0]):
        fc = far_c[g : g + 1]
        fs = far_s[g : g + 1]
        cos.append(near_c * fc - near_s * fs)
        sin.append(-(near_s * fc + near_c * fs))
    return jnp.concatenate([jnp.concatenate(cos, axis=0), jnp.concatenate(sin, axis=0)], axis=1)


def places(size, pup):
    return (lax.broadcasted_iota(jnp.int32, (1, size), 1).astype(F32) - (pup / 2 - 0.5)) * (1.0 / pup)


def mirror_surface(cmd_ref, infl_ref, half_refs):
    blocks = cmd_ref.shape[0]
    mirrors, acts, pup = infl_ref.shape
    per_block = cmd_ref.shape[2] // acts
    per_mirror = blocks // mirrors
    lefts = []
    for m in range(mirrors):
        halves = []
        for h in range(pup // LANES):
            half_ref = half_refs[m * (pup // LANES) + h]
            half_ref[...] = infl_ref[m, :, h * LANES : (h + 1) * LANES]
            halves.append([half_ref[pl.ds(a, per_mirror, stride=per_block), :] for a in range(per_block)])
        lefts.append(jnp.concatenate([jnp.concatenate(part, axis=0) for part in halves], axis=1))
    left_hi, left_lo = split2(jnp.concatenate(lefts, axis=0).T)
    rights = []
    for m in range(mirrors):
        part = jnp.concatenate([cmd_ref[m * per_mirror + j] for j in range(per_mirror)], axis=0)
        act_hi, act_lo = split2(jnp.concatenate([part[:, a * acts : (a + 1) * acts] for a in range(per_block)], axis=0))
        infl_hi, infl_lo = split2(infl_ref[m])
        both = mm(jnp.concatenate([act_hi, act_lo], axis=0), infl_hi)
        rights.append(both[:acts] + both[acts:] + mm(act_hi, infl_lo))
    right_hi, right_lo = split2(jnp.concatenate(rights, axis=0))
    both = mm(jnp.concatenate([left_hi, left_lo], axis=0), right_hi)
    return both[:pup] + both[pup:] + mm(left_hi, right_lo)


def turned(x):
    half = x.shape[1] // 2
    re = x[:, :half]
    im = x[:, half:]
    return jnp.concatenate([jnp.concatenate([re, -im], axis=1), jnp.concatenate([im, re], axis=1)], axis=0)


def check_scratch(waves):
    return [pltpu.SemaphoreType.DMA, pltpu.VMEM((PUP, PUP), F32)] + [pltpu.VMEM((ACT, LANES), F32)] * 4


def check_kernel(cmd_ref, infl_ref, aber_ref, amp_ref, wave_ref, mask_ref, all_ref, flip_ref, back_ref, out_ref, stat_ref, all_out, sem, height_ref, *half_refs):
    whole = pltpu.make_async_copy(all_ref, all_out, sem)
    whole.start()
    row = lax.axis_index("rows")
    col = lax.axis_index("cols")
    waves, band, full = out_ref.shape
    pup = aber_ref.shape[0]
    half = pup // 2
    side = full // 2
    groups_count = wave_ref.shape[0] // waves
    first_wave = (col % groups_count) * waves
    lane = lax.broadcasted_iota(jnp.int32, (1, LANES), 1)
    mask = mask_ref[...]
    stat = jnp.zeros((1, LANES), F32)
    near_u = lax.broadcasted_iota(jnp.int32, (8, 1), 0).astype(F32) - (full / 2 - 0.5)
    far_u = (lax.broadcasted_iota(jnp.int32, (side // 8, 1), 0) * 8).astype(F32)
    band_u = (lax.broadcasted_iota(jnp.int32, (band // 8, 1), 0) * 8 + row * band).astype(F32)
    flip = flip_ref[...]
    back = back_ref[...]
    inverse = []
    for w in range(waves):
        one = 1.0 / jnp.full((1, LANES), wave_ref[first_wave + w], F32)
        inverse.append(jnp.concatenate([one] * (pup // LANES), axis=1))

    def pupil(w):
        cos, sin = cos_sin_turns(height_ref[...] * inverse[w])
        amp = amp_ref[...]
        return split2(jnp.concatenate([amp * cos, amp * sin], axis=0))

    def band_table(w):
        hi, lo = split2(transform(near_u, band_u, places(pup, pup) * (PIXEL_SCALE * inverse[w])))
        return turned(hi), turned(lo)

    def half_table(w):
        return split2(transform(near_u, far_u, places(half, pup) * (PIXEL_SCALE * inverse[w][:, :half])))

    def near_side(table, held):
        pupil_hi, pupil_lo = held
        y_hi, y_lo = table
        return mm(jnp.concatenate([y_hi, y_lo], axis=0), pupil_hi), mm(y_hi, pupil_lo)

    def fold(up, low):
        up = up[: 2 * band] + up[2 * band :] + low
        upper_hi, upper_lo = split2(up[:, half:])
        return up[:, :half], mm(jnp.concatenate([upper_hi, upper_lo], axis=0), flip)

    def middle(lower, upper):
        upper = upper[: 2 * band] + upper[2 * band :]
        parts = []
        for even, odd in zip(split2(lower + upper), split2(lower - upper)):
            re = even[:band]
            im = even[band:]
            odd_re = odd[:band]
            odd_im = odd[band:]
            rows = [(re, -odd_im), (im, odd_re), (re, odd_im), (im, -odd_re)]
            parts.append(jnp.concatenate([jnp.concatenate(pair, axis=1) for pair in rows], axis=0))
        return parts

    def far_side(table, mid):
        mid_hi, mid_lo = mid
        hi, lo = table
        return mm_t(jnp.concatenate([mid_hi, mid_lo], axis=0), hi), mm_t(mid_hi, lo)

    def unfold(field, low):
        field = field[: 4 * band] + field[4 * band :] + low
        field = field * field
        near = field[:band] + field[band : 2 * band]
        near = jnp.concatenate([near, jnp.zeros((band, 2 * LANES - side), F32)], axis=1)
        far_hi, far_lo = split2(field[2 * band : 3 * band] + field[3 * band :])
        return near, mm(jnp.concatenate([far_hi, far_lo], axis=0), back)

    def finish(w, near, far, stat):
        far = far[:band] + far[band:]
        intensity = jnp.concatenate([near[:, :LANES], near[:, LANES:] + far[:, :LANES], far[:, LANES:]], axis=1)
        out_ref[w] = intensity
        total = jnp.sum(jnp.sum(intensity, axis=0, keepdims=True), axis=1, keepdims=True)
        hole = jnp.sum(jnp.sum(intensity * mask, axis=0, keepdims=True), axis=1, keepdims=True)
        stat = jnp.where(lane == w, total, stat)
        return jnp.where(lane == waves + w, hole, stat)

    height_ref[...] = aber_ref[...] + (2.0 * STROKE) * mirror_surface(cmd_ref, infl_ref, half_refs)
    first, folded, mid, field, image = {}, {}, {}, {}, {}
    for step in range(waves + 4):
        if step < waves:
            first[step] = near_side(band_table(step), pupil(step))
        w = step - 1
        if 0 <= w < waves:
            folded[w] = fold(*first.pop(w))
        w = step - 2
        if 0 <= w < waves:
            field[w] = far_side(half_table(w), middle(*folded.pop(w)))
        w = step - 3
        if 0 <= w < waves:
            image[w] = unfold(*field.pop(w))
        w = step - 4
        if 0 <= w < waves:
            stat = finish(w, *image.pop(w), stat)
    spread(stat_ref, stat)
    whole.wait()


def scale_kernel(stat_ref, int_ref, out_ref, contrast_ref, *, holes):
    waves = int_ref.shape[0]
    stat = gathered_sum(stat_ref)
    scale = stat[:, :waves] / (FP * FP) + EPSILON
    contrast_ref[...] = stat[:, waves : 2 * waves] / holes / scale
    inverse = 1.0 / scale
    for w in range(waves):
        out_ref[w] = int_ref[w] * inverse[:, w : w + 1]


def call(kernel, name, outs, args, scratch=(), smem=(), hbm=(), hbm_out=()):
    def space(i):
        return pltpu.SMEM if i in smem else pl.ANY if i in hbm else pltpu.VMEM

    return pl.pallas_call(
        kernel,
        out_shape=[jax.ShapeDtypeStruct(s, F32) if isinstance(s, tuple) else s for s in outs],
        in_specs=[pl.BlockSpec(memory_space=space(i)) for i in range(len(args))],
        out_specs=[pl.BlockSpec(memory_space=pl.ANY if i in hbm_out else pltpu.VMEM) for i in range(len(outs))],
        scratch_shapes=[pltpu.VMEM(s, F32) if isinstance(s, tuple) else s for s in scratch],
        compiler_params=pltpu.CompilerParams(vmem_limit_bytes=16 << 20),
        cost_estimate=pl.CostEstimate(flops=20_000_000_000, bytes_accessed=1 << 20, transcendentals=0),
        name=name,
    )(*args)


def exchange(x, axis):
    return lax.all_to_all(x, axis, 0, 0)


def on_device(estimate, dark_hole, jacobian, basis, eigenvalues, exponents, wavelengths, amplitude, aberration, influence):
    rows = lax.axis_size("rows")
    cols = lax.axis_size("cols")
    tile_rows, width = jacobian.shape
    modes = basis.shape[0]
    cands = exponents.shape[0]
    waves = wavelengths.shape[0] // (cols // cands)
    band = FP // rows
    holes = dark_hole.shape[0]
    matrices = [jax.ShapeDtypeStruct(s, BF16) for s in ((PUP // 2, PUP // 2), (FP // 2, 2 * LANES))]
    flip, back = call(reversal_kernel, "reversals", matrices, [])
    share, mask = call(
        pick_kernel, "pick", [(cols, 1, tile_rows), (band, FP)],
        [estimate, dark_hole.reshape(1, holes), flip],
        scratch=[(estimate.shape[1] // LANES, LANES), (band * FP // LANES, LANES)], hbm=(2,),
    )
    share = exchange(share, "cols")
    (grad,) = call(gradient_kernel, "gradient", [(rows, 1, width)], [share, jacobian])
    grad = exchange(grad, "rows")
    (modal,) = call(modal_kernel, "modal", [(cols, 1, modes)], [grad, basis])
    modal = exchange(modal, "cols")
    (parts,) = call(command_kernel, "commands", [(rows, LEVELS * width // LANES, LANES)], [modal, eigenvalues, basis])
    parts = exchange(parts, "rows")
    commands, chosen = call(
        gather_kernel, "gather", [(cands, width), (cols, 1, width)], [parts, exponents],
        scratch=[(LEVELS * width // LANES, 1, LANES)], smem=(1,),
    )
    chosen = exchange(chosen, "cols")
    intensity, stat, commands = call(
        check_kernel, "check", [(waves, band, FP), (rows, 1, LANES), (cands, width)],
        [chosen, jnp.swapaxes(influence, 1, 2), aberration, amplitude, wavelengths, mask, commands, flip, back],
        scratch=check_scratch(waves), smem=(4,), hbm_out=(2,),
    )
    stat = exchange(stat, "rows")
    image, contrast = call(
        functools.partial(scale_kernel, holes=holes), "scale", [(waves, band, FP), (1, waves)], [stat, intensity],
    )
    return commands, image, contrast


def solution(mesh):
    return jax.shard_map(
        on_device,
        mesh=mesh,
        in_specs=(
            P(None, "cols"),
            P(),
            P("rows", "cols"),
            P("rows", "cols"),
            P("rows"),
            P(),
            P(),
            P(),
            P(),
            P(),
        ),
        out_specs=(P(None, "cols"), P("cols", "rows", None), P("cols", None)),
        check_vma=False,
    )
```

```python
import functools

import jax
import jax.numpy as jnp
from jax import lax
from jax.experimental import pallas as pl
from jax.experimental.pallas import tpu as pltpu
from jax.sharding import PartitionSpec as P

FP = 384
PUP = 256
ACT = 96
LANES = 128
EPSILON = 1e-6
STROKE = 0.05
PIXEL_SCALE = 0.25
F32 = jnp.float32
BF16 = jnp.bfloat16
LEAST = -2
LEVELS = 6
HIGHEST = lax.Precision.HIGHEST

COS = (0.9999992251396179, -19.738981246948242, 64.92865753173828, -85.27162170410156, 58.79049301147461, -21.07110595703125)
SIN = (6.283185005187988, -41.341590881347656, 81.59994506835938, -76.61447143554688, 41.3428840637207, -12.471243858337402)


def horner(coefs, x):
    acc = jnp.full_like(x, coefs[-1])
    for c in coefs[-2::-1]:
        acc = acc * x + c
    return acc


def cos_sin_turns(t):
    r = t - jnp.round(t)
    x = r * r
    return horner(COS, x), horner(SIN, x) * r


def split2(x):
    hi = x.astype(BF16)
    return hi, (x - hi.astype(F32)).astype(BF16)


def mm(a, b):
    return jnp.dot(a, b, preferred_element_type=F32)


def mm_t(a, b, precision=None):
    return lax.dot_general(a, b, (((1,), (1,)), ((), ())), preferred_element_type=F32, precision=precision)


def tdot(a, b, precision=None):
    return lax.dot_general(a, b, (((0,), (0,)), ((), ())), preferred_element_type=F32, precision=precision)


def spread(ref, row):
    for j in range(ref.shape[0]):
        ref[j] = row


def gathered_sum(ref):
    total = ref[0]
    for j in range(1, ref.shape[0]):
        total = total + ref[j]
    return total


def reversal_kernel(flip_ref, back_ref):
    half = flip_ref.shape[0]
    side, wide = back_ref.shape
    i = lax.broadcasted_iota(jnp.int32, (half, half), 0)
    j = lax.broadcasted_iota(jnp.int32, (half, half), 1)
    flip_ref[...] = (i + j == half - 1).astype(F32).astype(BF16)
    i = lax.broadcasted_iota(jnp.int32, (side, wide), 0)
    j = lax.broadcasted_iota(jnp.int32, (side, wide), 1)
    back_ref[...] = (i + j == wide - 1).astype(F32).astype(BF16)


def one_hot(rows, index):
    held = jnp.clip(index, -1, 255).astype(F32).astype(BF16)
    row = lax.broadcasted_iota(jnp.int32, (rows, 1), 0).astype(F32).astype(BF16)
    return jnp.where(row == held, jnp.ones((), BF16), jnp.zeros((), BF16))


def pick_kernel(est_ref, dh_ref, after_ref, out_ref, mask_ref, plane_ref, flat_ref):
    row = lax.axis_index("rows")
    col = lax.axis_index("cols")
    planes, width = est_ref.shape
    groups = width // LANES
    count = out_ref.shape[-1]
    per_plane = lax.axis_size("rows") // planes
    offset = pl.multiple_of((row % per_plane) * count, LANES)
    ours = lax.broadcasted_iota(jnp.int32, (planes, 1), 0) == row // per_plane
    plane = jnp.sum(jnp.where(ours, est_ref[...], 0.0), axis=0, keepdims=True)
    for j in range(groups):
        plane_ref[j : j + 1, :] = plane[:, j * LANES : (j + 1) * LANES]
    hi, lo = split2(plane_ref[...])
    place = dh_ref[:, pl.ds(offset, count)] - col * (groups * LANES)
    chosen = one_hot(groups, place >> 7)
    found = tdot(hi, chosen) + tdot(lo, chosen)
    keep = lax.broadcasted_iota(jnp.int32, (LANES, count), 0) == (place & (LANES - 1))
    spread(out_ref, jnp.sum(jnp.where(keep, found, 0.0), axis=0, keepdims=True))
    band, full = mask_ref.shape
    per_row = full // LANES
    pix = dh_ref[...] - row * (band * full)
    flat_ref[...] = mm_t(one_hot(band * per_row, pix >> 7), one_hot(LANES, pix & (LANES - 1)))
    for j in range(per_row):
        mask_ref[:, j * LANES : (j + 1) * LANES] = flat_ref[pl.ds(j, band, stride=per_row), :]


def gradient_kernel(field_ref, jac_ref, out_ref):
    field = gathered_sum(field_ref)
    tile_rows, width = jac_ref.shape
    tiles = width // LANES
    acc = [jnp.zeros((8, LANES), F32) for _ in range(tiles)]
    for b in range(tile_rows // LANES):
        block = jnp.broadcast_to(field[:, b * LANES : (b + 1) * LANES], (LANES, LANES)).T
        for s in range(LANES // 8):
            scale = block[s * 8 : s * 8 + 8]
            at = b * LANES + s * 8
            for l in range(tiles):
                acc[l] = acc[l] + scale * jac_ref[at : at + 8, l * LANES : (l + 1) * LANES]
    row = jnp.concatenate([jnp.sum(a, axis=0, keepdims=True) for a in acc], axis=1)
    spread(out_ref, row)


def modal_kernel(grad_ref, basis_ref, out_ref):
    grad = gathered_sum(grad_ref)
    tile_rows, width = basis_ref.shape
    tiles = width // LANES
    lanes = [jnp.broadcast_to(grad[:, l * LANES : (l + 1) * LANES], (8, LANES)) for l in range(tiles)]
    parts = []
    for b in range(tile_rows // LANES):
        pieces = []
        for s in range(LANES // 8):
            at = b * LANES + s * 8
            acc = lanes[0] * basis_ref[at : at + 8, 0:LANES]
            for l in range(1, tiles):
                acc = acc + lanes[l] * basis_ref[at : at + 8, l * LANES : (l + 1) * LANES]
            pieces.append(acc)
        parts.append(jnp.sum(jnp.concatenate(pieces, axis=0).T, axis=0, keepdims=True))
    spread(out_ref, jnp.concatenate(parts, axis=1))


def command_kernel(modal_ref, eig_ref, basis_ref, out_ref):
    modal = gathered_sum(modal_ref)
    eigen = eig_ref[...].reshape(modal.shape)
    tile_rows, width = basis_ref.shape
    step = 256
    rows = 8
    damping = jnp.exp2((lax.broadcasted_iota(jnp.int32, (rows, 1), 0) + LEAST).astype(F32))
    acc = jnp.zeros((2 * rows, width), F32)
    for b in range(tile_rows // step):
        at = slice(b * step, (b + 1) * step)
        weights = -modal[:, at] / (eigen[:, at] + damping)
        high = weights.astype(BF16).astype(F32)
        both = jnp.concatenate([high, weights - high], axis=0).astype(BF16)
        hi, lo = split2(basis_ref[at, :])
        acc = acc + mm(both, hi) + mm(both, lo)
    levels = acc[:rows] + acc[rows:]
    spread(out_ref, jnp.concatenate([levels[l : l + 1] for l in range(LEVELS)], axis=1))


def gather_kernel(parts_ref, exp_ref, out_ref, send_ref, levels_ref):
    levels_ref[...] = gathered_sum(parts_ref)
    cands, width = out_ref.shape
    copies = send_ref.shape[0] // cands
    for k in range(cands):
        level = exp_ref[k] - LEAST
        row = levels_ref[:, pl.ds(pl.multiple_of(level * width, LANES), width)]
        out_ref[k : k + 1, :] = row
        for j in range(copies):
            send_ref[k * copies + j] = row


def transform(near_u, far_u, turns):
    near_c, near_s = cos_sin_turns(near_u * turns)
    far_c, far_s = cos_sin_turns(far_u * turns)
    cos = []
    sin = []
    for g in range(far_u.shape[0]):
        fc = far_c[g : g + 1]
        fs = far_s[g : g + 1]
        cos.append(near_c * fc - near_s * fs)
        sin.append(-(near_s * fc + near_c * fs))
    return jnp.concatenate([jnp.concatenate(cos, axis=0), jnp.concatenate(sin, axis=0)], axis=1)


def places(size, pup):
    return (lax.broadcasted_iota(jnp.int32, (1, size), 1).astype(F32) - (pup / 2 - 0.5)) * (1.0 / pup)


def mirror_surface(cmd_ref, infl_ref, half_refs):
    blocks = cmd_ref.shape[0]
    mirrors, acts, pup = infl_ref.shape
    per_block = cmd_ref.shape[2] // acts
    per_mirror = blocks // mirrors
    lefts = []
    for m in range(mirrors):
        halves = []
        for h in range(pup // LANES):
            half_ref = half_refs[m * (pup // LANES) + h]
            half_ref[...] = infl_ref[m, :, h * LANES : (h + 1) * LANES]
            halves.append([half_ref[pl.ds(a, per_mirror, stride=per_block), :] for a in range(per_block)])
        lefts.append(jnp.concatenate([jnp.concatenate(part, axis=0) for part in halves], axis=1))
    left_hi, left_lo = split2(jnp.concatenate(lefts, axis=0).T)
    rights = []
    for m in range(mirrors):
        part = jnp.concatenate([cmd_ref[m * per_mirror + j] for j in range(per_mirror)], axis=0)
        act_hi, act_lo = split2(jnp.concatenate([part[:, a * acts : (a + 1) * acts] for a in range(per_block)], axis=0))
        infl_hi, infl_lo = split2(infl_ref[m])
        both = mm(jnp.concatenate([act_hi, act_lo], axis=0), infl_hi)
        rights.append(both[:acts] + both[acts:] + mm(act_hi, infl_lo))
    right_hi, right_lo = split2(jnp.concatenate(rights, axis=0))
    both = mm(jnp.concatenate([left_hi, left_lo], axis=0), right_hi)
    return both[:pup] + both[pup:] + mm(left_hi, right_lo)


def turned(x):
    half = x.shape[1] // 2
    re = x[:, :half]
    im = x[:, half:]
    return jnp.concatenate([jnp.concatenate([re, -im], axis=1), jnp.concatenate([im, re], axis=1)], axis=0)


def check_scratch(waves):
    return [pltpu.SemaphoreType.DMA, pltpu.VMEM((PUP, PUP), F32)] + [pltpu.VMEM((ACT, LANES), F32)] * 4


def check_kernel(cmd_ref, infl_ref, aber_ref, amp_ref, wave_ref, mask_ref, all_ref, flip_ref, back_ref, out_ref, stat_ref, all_out, sem, height_ref, *half_refs):
    whole = pltpu.make_async_copy(all_ref, all_out, sem)
    whole.start()
    row = lax.axis_index("rows")
    col = lax.axis_index("cols")
    waves, band, full = out_ref.shape
    pup = aber_ref.shape[0]
    half = pup // 2
    side = full // 2
    groups_count = wave_ref.shape[0] // waves
    first_wave = (col % groups_count) * waves
    lane = lax.broadcasted_iota(jnp.int32, (1, LANES), 1)
    mask = mask_ref[...]
    stat = jnp.zeros((1, LANES), F32)
    near_u = lax.broadcasted_iota(jnp.int32, (8, 1), 0).astype(F32) - (full / 2 - 0.5)
    far_u = (lax.broadcasted_iota(jnp.int32, (side // 8, 1), 0) * 8).astype(F32)
    band_u = (lax.broadcasted_iota(jnp.int32, (band // 8, 1), 0) * 8 + row * band).astype(F32)
    flip = flip_ref[...]
    back = back_ref[...]
    inverse = []
    for w in range(waves):
        one = 1.0 / jnp.full((1, LANES), wave_ref[first_wave + w], F32)
        inverse.append(jnp.concatenate([one] * (pup // LANES), axis=1))

    def pupil(w):
        cos, sin = cos_sin_turns(height_ref[...] * inverse[w])
        amp = amp_ref[...]
        return split2(jnp.concatenate([amp * cos, amp * sin], axis=0))

    def band_table(w):
        hi, lo = split2(transform(near_u, band_u, places(pup, pup) * (PIXEL_SCALE * inverse[w])))
        return turned(hi), turned(lo)

    def half_table(w):
        return split2(transform(near_u, far_u, places(half, pup) * (PIXEL_SCALE * inverse[w][:, :half])))

    def near_side(table, held):
        pupil_hi, pupil_lo = held
        y_hi, y_lo = table
        return mm(jnp.concatenate([y_hi, y_lo], axis=0), pupil_hi), mm(y_hi, pupil_lo)

    def fold(up, low):
        up = up[: 2 * band] + up[2 * band :] + low
        upper_hi, upper_lo = split2(up[:, half:])
        return up[:, :half], mm(jnp.concatenate([upper_hi, upper_lo], axis=0), flip)

    def middle(lower, upper):
        upper = upper[: 2 * band] + upper[2 * band :]
        parts = []
        for even, odd in zip(split2(lower + upper), split2(lower - upper)):
            re = even[:band]
            im = even[band:]
            odd_re = odd[:band]
            odd_im = odd[band:]
            rows = [(re, -odd_im), (im, odd_re), (re, odd_im), (im, -odd_re)]
            parts.append(jnp.concatenate([jnp.concatenate(pair, axis=1) for pair in rows], axis=0))
        return parts

    def far_side(table, mid):
        mid_hi, mid_lo = mid
        hi, lo = table
        return mm_t(jnp.concatenate([mid_hi, mid_lo], axis=0), hi), mm_t(mid_hi, lo)

    def unfold(field, low):
        field = field[: 4 * band] + field[4 * band :] + low
        field = field * field
        near = field[:band] + field[band : 2 * band]
        near = jnp.concatenate([near, jnp.zeros((band, 2 * LANES - side), F32)], axis=1)
        far_hi, far_lo = split2(field[2 * band : 3 * band] + field[3 * band :])
        return near, mm(jnp.concatenate([far_hi, far_lo], axis=0), back)

    def finish(w, near, far, stat):
        far = far[:band] + far[band:]
        intensity = jnp.concatenate([near[:, :LANES], near[:, LANES:] + far[:, :LANES], far[:, LANES:]], axis=1)
        out_ref[w] = intensity
        total = jnp.sum(jnp.sum(intensity, axis=0, keepdims=True), axis=1, keepdims=True)
        hole = jnp.sum(jnp.sum(intensity * mask, axis=0, keepdims=True), axis=1, keepdims=True)
        stat = jnp.where(lane == w, total, stat)
        return jnp.where(lane == waves + w, hole, stat)

    height_ref[...] = aber_ref[...] + (2.0 * STROKE) * mirror_surface(cmd_ref, infl_ref, half_refs)
    first, folded, mid, field, image = {}, {}, {}, {}, {}
    for step in range(waves + 4):
        if step < waves:
            first[step] = near_side(band_table(step), pupil(step))
        w = step - 1
        if 0 <= w < waves:
            folded[w] = fold(*first.pop(w))
        w = step - 2
        if 0 <= w < waves:
            field[w] = far_side(half_table(w), middle(*folded.pop(w)))
        w = step - 3
        if 0 <= w < waves:
            image[w] = unfold(*field.pop(w))
        w = step - 4
        if 0 <= w < waves:
            stat = finish(w, *image.pop(w), stat)
    spread(stat_ref, stat)
    whole.wait()


def scale_kernel(stat_ref, int_ref, out_ref, contrast_ref, *, holes):
    waves = int_ref.shape[0]
    stat = gathered_sum(stat_ref)
    scale = stat[:, :waves] / (FP * FP) + EPSILON
    contrast_ref[...] = stat[:, waves : 2 * waves] / holes / scale
    inverse = 1.0 / scale
    for w in range(waves):
        out_ref[w] = int_ref[w] * inverse[:, w : w + 1]


def call(kernel, name, outs, args, scratch=(), smem=(), hbm=(), hbm_out=()):
    def space(i):
        return pltpu.SMEM if i in smem else pl.ANY if i in hbm else pltpu.VMEM

    return pl.pallas_call(
        kernel,
        out_shape=[jax.ShapeDtypeStruct(s, F32) if isinstance(s, tuple) else s for s in outs],
        in_specs=[pl.BlockSpec(memory_space=space(i)) for i in range(len(args))],
        out_specs=[pl.BlockSpec(memory_space=pl.ANY if i in hbm_out else pltpu.VMEM) for i in range(len(outs))],
        scratch_shapes=[pltpu.VMEM(s, F32) if isinstance(s, tuple) else s for s in scratch],
        compiler_params=pltpu.CompilerParams(vmem_limit_bytes=16 << 20),
        cost_estimate=pl.CostEstimate(flops=20_000_000_000, bytes_accessed=1 << 20, transcendentals=0),
        name=name,
    )(*args)


def exchange(x, axis):
    return lax.all_to_all(x, axis, 0, 0)


def on_device(estimate, dark_hole, jacobian, basis, eigenvalues, exponents, wavelengths, amplitude, aberration, influence):
    rows = lax.axis_size("rows")
    cols = lax.axis_size("cols")
    tile_rows, width = jacobian.shape
    modes = basis.shape[0]
    cands = exponents.shape[0]
    waves = wavelengths.shape[0] // (cols // cands)
    band = FP // rows
    holes = dark_hole.shape[0]
    matrices = [jax.ShapeDtypeStruct(s, BF16) for s in ((PUP // 2, PUP // 2), (FP // 2, 2 * LANES))]
    flip, back = call(reversal_kernel, "reversals", matrices, [])
    share, mask = call(
        pick_kernel, "pick", [(cols, 1, tile_rows), (band, FP)],
        [estimate, dark_hole.reshape(1, holes), flip],
        scratch=[(estimate.shape[1] // LANES, LANES), (band * FP // LANES, LANES)], hbm=(2,),
    )
    share = exchange(share, "cols")
    (grad,) = call(gradient_kernel, "gradient", [(rows, 1, width)], [share, jacobian])
    grad = exchange(grad, "rows")
    (modal,) = call(modal_kernel, "modal", [(cols, 1, modes)], [grad, basis])
    modal = exchange(modal, "cols")
    (parts,) = call(command_kernel, "commands", [(rows, 1, LEVELS * width)], [modal, eigenvalues, basis])
    parts = exchange(parts, "rows")
    commands, chosen = call(
        gather_kernel, "gather", [(cands, width), (cols, 1, width)], [parts, exponents],
        scratch=[(1, LEVELS * width)], smem=(1,),
    )
    chosen = exchange(chosen, "cols")
    intensity, stat, commands = call(
        check_kernel, "check", [(waves, band, FP), (rows, 1, LANES), (cands, width)],
        [chosen, jnp.swapaxes(influence, 1, 2), aberration, amplitude, wavelengths, mask, commands, flip, back],
        scratch=check_scratch(waves), smem=(4,), hbm_out=(2,),
    )
    stat = exchange(stat, "rows")
    image, contrast = call(
        functools.partial(scale_kernel, holes=holes), "scale", [(waves, band, FP), (1, waves)], [stat, intensity],
    )
    return commands, image, contrast


def solution(mesh):
    return jax.shard_map(
        on_device,
        mesh=mesh,
        in_specs=(
            P(None, "cols"),
            P(),
            P("rows", "cols"),
            P("rows", "cols"),
            P("rows"),
            P(),
            P(),
            P(),
            P(),
            P(),
        ),
        out_specs=(P(None, "cols"), P("cols", "rows", None), P("cols", None)),
        check_vma=False,
    )
```
